128 devices in a mesh: rx: 16 (over z, x), ry: 8 (over y, core).
Axes of the slice: x: 4, y: 4, z: 4, core: 2. Of those that a mesh axis runs over, the one named last changes fastest.
Arguments:
- anchors: float32 [3, 49152], P(None, ('rx', 'ry')), may hold values from -6 to 6
- directions: float32 [3, 49152], P(None, ('rx', 'ry')), may hold values from -3 to 3
- regions: int32 [49152, 4], P(('rx', 'ry')), may hold values from 0 to 127, all different within a row; in each aligned block of 384 rows (0 to 383, 384 to 767, ...) at most 24 rows name the same one
- counts: int32 [49152, 4], P(('rx', 'ry')), may hold values from 1 to 16
- seg_len: float32 [4, 49152], P(None, ('rx', 'ry')), may hold values from 0.25 to 2
- color_grad: float32 [3, 49152], P(None, ('rx', 'ry')), may hold values from -6 to 6
- frequencies: float32 [128, 3, 128], P(('rx', 'ry')), may hold values from -9 to 9
- w_hidden: bfloat16 [128, 256, 256], P(('rx', 'ry')), may hold values from -0.375 to 0.375
- b_hidden: float32 [128, 256], P(('rx', 'ry')), may hold values from -3 to 3
- w_out: bfloat16 [128, 4, 256], P(('rx', 'ry')), may hold values from -0.375 to 0.375
- b_out: float32 [128, 4], P(('rx', 'ry')), may hold values from -4 to 4
Outputs:
- colour: float32 [3, 49152], P(None, ('rx', 'ry'))
- grad_hidden: float32 [128, 256, 256], P(('rx', 'ry'))
- grad_hidden_bias: float32 [128, 256], P(('rx', 'ry'))
- grad_out: float32 [128, 4, 256], P(('rx', 'ry'))
- grad_out_bias: float32 [128, 4], P(('rx', 'ry'))
The draws below stay inside these ranges and needn't reach their ends.
Inputs may be any that keep to these rules, and one draw needn't show every extreme that they name: Each ray names 4 different regions; among the rays of one device no region is named by more than 24 segments, and some region reaches 24.
All inputs are finite; a program needn't handle non-finite values.
Results may differ from the reference program's by a relative error of at most 0.0027.
Values sent between devices are 32-bit elements; how exact they have to be, the bound alone decides.
No kernel may reach another device: no remote copies, remote signals or barrier semaphores. Data moves between devices by JAX's collectives and lax.ppermute only.
A program may use at most 64 MiB of HBM per device.

```python
import math
import jax
import jax.numpy as jnp
import numpy as np
from jax import lax

WIDTH = 256
HALF = 128
K = 4
S = 16
RAY_DEV = 384
REGIONS = 128
MOST = 24
RAYS = 49152
N_RX = 16
N_RY = 8


def with_ends(entries, key, low, largest):
    longest = entries.shape.index(max(entries.shape))
    spots = []
    for shift in (0, 1):
        where = [jax.random.randint(jax.random.fold_in(key, axis), (), 0, length) for axis, length in enumerate(entries.shape)]
        where[longest] = (where[longest] + shift) % entries.shape[longest]
        spots.append(tuple(where))
    return entries.at[spots[0]].set(low).at[spots[1]].set(largest)


def block_levels(rng, extent, cuts, least, largest):
    loudness = 1.0
    for axis_at, blocks in cuts:
        draws = jax.random.uniform(jax.random.fold_in(jax.random.fold_in(rng, 6), axis_at), (blocks,), jnp.float32, least / len(cuts), largest / len(cuts))
        loudness = loudness * jnp.repeat(jnp.exp(draws), extent[axis_at] // blocks).reshape((-1,) + (1,) * (len(extent) - 1 - axis_at))
    return loudness


def shared_out(rng, own, number, rows, count, top, most, skew):
    ranking = jax.random.permutation(rng, count)
    packed, ordinary = portions_of(count, rows * top, most, skew, True), portions_of(count, rows * top, most, skew, False)
    places = jnp.arange(count)

    def named(sizes, rotation):
        used = int((sizes > 0).sum())
        fixed = max(1, used // 4)
        moved = fixed + (places - fixed + rotation * (used - fixed)) % max(1, count - fixed)
        return jnp.zeros((count,), jnp.int32).at[ranking[jnp.where(places < fixed, places, moved)]].set(jnp.asarray(sizes, jnp.int32))

    sizes = jnp.where(number % 4 == 0, named(packed, number // 4), named(ordinary, number - number // 4 - 1))
    mixed = jax.random.permutation(jax.random.fold_in(own, 3), count)
    donor, receiver = mixed[0:count // 2 * 2:2], mixed[1:count // 2 * 2:2]
    slack = jnp.minimum(sizes[donor] - 1, most - sizes[receiver]) // 2
    slack = jnp.where((donor == ranking[0]) | (receiver == ranking[0]) | (sizes[receiver] == 0), 0, jnp.maximum(slack, 0))
    moved = jax.random.randint(jax.random.fold_in(own, 4), (count // 2,), 0, 1 << 20) % (slack + 1)
    sizes = sizes.at[donor].add(-moved).at[receiver].add(moved)
    labels = jnp.searchsorted(jnp.cumsum(sizes), jnp.arange(rows * top), side="right").astype(jnp.int32)
    grid = labels.reshape(top, rows).T
    grid = grid[jax.random.permutation(jax.random.fold_in(own, 1), rows)]
    rotation = jax.random.randint(jax.random.fold_in(own, 2), (rows, 1), 0, top)
    return jnp.take_along_axis(grid, (jnp.arange(top)[None, :] + rotation) % top, axis=1)


def portions_of(count, total, most, lean, full):
    weights = [(1 << 20) // math.isqrt(rank ** lean) + 1 for rank in range(1, count + 1)]
    largest = most if full else min(most, max(-(-total // count), total * weights[0] // sum(weights)))
    least = 1 if total - largest >= count - 1 else 0
    holding, rest = [largest] + [least] * (count - 1), total - largest - least * (count - 1)
    while rest > 0:
        free = [i for i in range(1, count) if holding[i] < largest] or [i for i in range(1, count) if holding[i] < most]
        pool, budget = sum([weights[i] for i in free]), rest
        for i in free:
            addition = min(most - holding[i], max(1, budget * weights[i] // pool), rest)
            holding[i] = holding[i] + addition
            rest = rest - addition
    return np.array(holding)


def noise(stream_key, extent, scale, reach, shards=(), kind=jnp.bfloat16):
    result = jax.random.normal(stream_key, extent, jnp.float32) * scale
    if len(shards) > 0:
        result = block_levels(stream_key, extent, shards, -0.22, 0.18) * result
    return jnp.clip(result, min=-reach, max=reach).astype(kind)


def setup_inputs(seed: int = 0) -> dict:
    streams_of = jax.random.split(jax.random.key(seed), 12)
    anchors = noise(streams_of[0], (3, RAYS), 1.0, 6.0, ((1, 128),), jnp.float32)
    directions = noise(streams_of[1], (3, RAYS), 0.5, 3.0, ((1, 128),), jnp.float32)
    regions_keys = jax.random.split(jax.random.fold_in(streams_of[2], 1), RAYS // RAY_DEV)
    regions_turns = jax.random.permutation(jax.random.fold_in(streams_of[2], 3), RAYS // RAY_DEV)
    regions = jax.vmap(lambda own, number: shared_out(jax.random.fold_in(streams_of[2], 2), own, number, RAY_DEV, N_RX * N_RY, K, MOST, 2))(regions_keys, regions_turns).reshape((RAYS, K))
    counts = with_ends(jax.random.randint(streams_of[3], (RAYS, K), 1, S + 1), jax.random.fold_in(streams_of[3], 1), 1, S).astype(jnp.int32)
    seg_len = jnp.clip(jnp.exp(math.log(2.0) - 2.0794415 * jax.random.uniform(streams_of[4], (K, RAYS), jnp.float32) ** block_levels(streams_of[4], (K, RAYS), ((1, 128),), -0.2, 0.2)), 0.25, 2.0)
    color_grad = noise(streams_of[5], (3, RAYS), 1.0, 6.0, ((1, 128),), jnp.float32)
    frequencies = noise(streams_of[6], (REGIONS, 3, HALF), 1.5, 9.0, ((0, 128),), jnp.float32)
    w_hidden = noise(streams_of[7], (REGIONS, WIDTH, WIDTH), WIDTH ** -0.5, 0.375, ((0, 128),))
    b_hidden = noise(streams_of[8], (REGIONS, WIDTH), 0.5, 3.0, ((0, 128),), jnp.float32)
    w_out = noise(streams_of[9], (REGIONS, 4, WIDTH), WIDTH ** -0.5, 0.375, ((0, 128),))
    b_out = noise(streams_of[10], (REGIONS, 4), 1.0, 4.0, ((0, 128),), jnp.float32)
    return {"anchors": anchors, "directions": directions, "regions": regions, "counts": counts, "seg_len": seg_len, "color_grad": color_grad, "frequencies": frequencies, "w_hidden": w_hidden, "b_hidden": b_hidden, "w_out": w_out, "b_out": b_out}


def slot_ranks(targets, region_count):
    one_hot = (targets[:, None] == jnp.arange(region_count, dtype=jnp.int32)[None, :]).astype(jnp.int32)
    before = jnp.cumsum(one_hot, axis=0) - one_hot
    return lax.optimization_barrier(jnp.sum(before * one_hot, axis=1)).astype(jnp.int32)

def request_fields(anchors, directions, counts, seg_len):
    ray_count, seg_count = counts.shape
    starts = 0.5 + jnp.cumsum(seg_len, axis=0) - seg_len

    def per_segment(array):
        rows = array.shape[0]
        return jnp.broadcast_to(array[:, :, None], (rows, ray_count, seg_count)).reshape(rows, ray_count * seg_count)
    return jnp.concatenate([per_segment(anchors), per_segment(directions), starts.T.reshape(1, -1), seg_len.T.reshape(1, -1), counts.astype(jnp.float32).reshape(1, -1)], axis=0)

def sample_steps(requests, samples):
    live_count = requests[8]
    spacing_row = requests[7] / jnp.maximum(live_count, 1.0)
    offsets = jnp.arange(samples, dtype=jnp.float32)[:, None] + 0.5
    sample_times = requests[6][None, :] + spacing_row[None, :] * offsets
    spacing = jnp.where(offsets < live_count[None, :], spacing_row[None, :] + jnp.zeros_like(sample_times), jnp.zeros_like(sample_times))
    return (sample_times, spacing)

def encode(requests, time_row, frequency):
    points = requests[0:3] + requests[3:6] * time_row[None, :]
    phases = points[0][:, None] * frequency[0][None, :] + points[1][:, None] * frequency[1][None, :] + points[2][:, None] * frequency[2][None, :]
    return jnp.concatenate([jnp.sin(phases), jnp.cos(phases)], axis=1).astype(jnp.bfloat16)

def hidden_layer(encoded, weight_hidden, bias_hidden):
    preact = jnp.dot(encoded, weight_hidden, preferred_element_type=jnp.float32) + bias_hidden[None, :]
    return (preact, jax.nn.silu(preact).astype(jnp.bfloat16))

def region_forward(requests, frequency, weight_hidden, bias_hidden, weight_out, bias_out, samples):
    sample_times, spacing = sample_steps(requests, samples)

    def one_row(time_row):
        preact, hidden = hidden_layer(encode(requests, time_row, frequency), weight_hidden, bias_hidden)
        outputs = lax.dot_general(weight_out, hidden, (((1,), (1,)), ((), ())), preferred_element_type=jnp.float32) + bias_out[:, None]
        return jnp.concatenate([jax.nn.softplus(outputs[0:1]), jax.nn.sigmoid(outputs[1:4])], axis=0)
    values = jnp.transpose(lax.map(one_row, sample_times), (1, 0, 2))
    return (values, sample_times, spacing)

def region_backward(requests, sample_times, values, pulls, frequency, weight_hidden, bias_hidden, weight_out):
    d_outputs = jnp.concatenate([pulls[0:1] * -jnp.expm1(-values[0:1]), pulls[1:4] * values[1:4] * (1.0 - values[1:4])], axis=0)
    width = weight_hidden.shape[0]

    def one_row(totals, row_pair):
        grad_h, grad_b, grad_o = totals
        time_row, d_row = row_pair
        encoded = encode(requests, time_row, frequency)
        preact, hidden = hidden_layer(encoded, weight_hidden, bias_hidden)
        d_rounded = d_row.astype(jnp.bfloat16)
        grad_o = grad_o + lax.dot_general(d_rounded, hidden, (((1,), (0,)), ((), ())), preferred_element_type=jnp.float32)
        d_hidden = lax.dot_general(d_rounded, weight_out, (((0,), (0,)), ((), ())), preferred_element_type=jnp.float32)
        squash = jax.nn.sigmoid(preact)
        d_pre = d_hidden * squash * (1.0 + preact * (1.0 - squash))
        grad_h = grad_h + lax.dot_general(encoded, d_pre.astype(jnp.bfloat16), (((0,), (0,)), ((), ())), preferred_element_type=jnp.float32)
        grad_b = grad_b + lax.optimization_barrier(jnp.sum(d_pre, axis=0))
        return ((grad_h, grad_b, grad_o), None)
    zeros_init = (jnp.zeros((width, width), jnp.float32), jnp.zeros((width,), jnp.float32), jnp.zeros((4, width), jnp.float32))
    totals, _ = lax.scan(one_row, zeros_init, (sample_times, jnp.transpose(d_outputs, (1, 0, 2))))
    return (totals[0], totals[1], totals[2], lax.optimization_barrier(jnp.sum(d_outputs, axis=(1, 2))))

def composite(sigma, colors, spacing):
    optical = sigma * spacing
    before = jnp.cumsum(optical, axis=0) - optical
    weight = jnp.exp(-before) * -jnp.expm1(-optical)
    return lax.optimization_barrier(jnp.sum(weight[None] * colors, axis=1))

def to_rays(array, seg_count):
    rows, samples, total = array.shape
    ray_count = total // seg_count
    return jnp.transpose(array.reshape(rows, samples, ray_count, seg_count), (0, 3, 1, 2)).reshape(rows, seg_count * samples, ray_count)

def from_rays(array, seg_count, samples):
    rows, _, ray_count = array.shape
    return jnp.transpose(array.reshape(rows, seg_count, samples, ray_count), (0, 2, 3, 1)).reshape(rows, samples, ray_count * seg_count)

def reference(anchors, directions, regions, counts, seg_len, color_grad, frequencies, w_hidden, b_hidden, w_out, b_out):
    region_count = N_RX * N_RY
    slot_total = region_count * MOST
    owner_targets = regions.reshape(region_count, RAY_DEV * K)
    ranks = lax.map(lambda targets: slot_ranks(targets, region_count), owner_targets)
    owner_index = jnp.arange(region_count, dtype=jnp.int32)[:, None]
    slot_index = (owner_targets * slot_total + owner_index * MOST + ranks).reshape(-1).astype(jnp.int32)
    requests = request_fields(anchors, directions, counts, seg_len)
    placed = jnp.zeros((9, region_count * slot_total), jnp.float32).at[:, slot_index].set(requests)
    per_region = jnp.transpose(placed.reshape(9, region_count, slot_total), (1, 0, 2))

    def forward_one(bundle):
        values, _, _ = region_forward(bundle[0], bundle[1], bundle[2], bundle[3], bundle[4], bundle[5], S)
        return values
    values = lax.map(forward_one, (per_region, frequencies, w_hidden, b_hidden, w_out, b_out))
    flat = jnp.transpose(values, (1, 2, 0, 3)).reshape(4 * S, region_count * slot_total)
    own_values = flat[:, slot_index]
    spacing = sample_steps(requests, S)[1]
    ray_spacing = to_rays(spacing[None], K)[0]
    ray_values = to_rays(own_values.reshape(4, S, RAYS * K), K)
    colour, ray_pull = jax.vjp(lambda sigma_in, colour_in: composite(sigma_in, colour_in, ray_spacing), ray_values[0], ray_values[1:4])
    d_sigma, d_colors = ray_pull(color_grad)
    replies = from_rays(jnp.concatenate([d_sigma[None], d_colors], axis=0), K, S).reshape(4 * S, RAYS * K)
    returned = jnp.zeros((4 * S, region_count * slot_total), jnp.float32).at[:, slot_index].set(replies)
    region_pulls = jnp.transpose(returned.reshape(4, S, region_count, slot_total), (2, 0, 1, 3))

    def backward_one(bundle):
        sample_times = sample_steps(bundle[0], S)[0]
        return region_backward(bundle[0], sample_times, bundle[1], bundle[2], bundle[3], bundle[4], bundle[5], bundle[6])
    grads = lax.map(backward_one, (per_region, values, region_pulls, frequencies, w_hidden, b_hidden, w_out))
    return (colour, grads[0], grads[1], grads[2], grads[3])
```

```python
import jax
import jax.numpy as jnp
from jax import lax
from jax.experimental import pallas as pl
from jax.experimental.pallas import tpu as pltpu
from jax.sharding import PartitionSpec as P

S = 16
K = 4
SLOTS = 24
PAD = 32
LANES = 128
BOTH = ("rx", "ry")
F32 = jnp.float32
BF16 = jnp.bfloat16
SIN = (3.14159264, -5.16771009, 2.55007766, -0.59829216, 0.07765941)
COS = (0.99999995, -4.93479286, 4.05841191, -1.33188016, 0.21969679)
TURN = 0.15915494309189535


def iota(shape, axis):
    return lax.broadcasted_iota(jnp.int32, shape, axis)


def nt(a, b):
    return lax.dot_general(a, b, (((1,), (1,)), ((), ())), preferred_element_type=F32)


def nn(a, b):
    return lax.dot_general(a, b, (((1,), (0,)), ((), ())), preferred_element_type=F32)


def split3(x):
    hi = x.astype(BF16).astype(F32)
    rest = x - hi
    mid = rest.astype(BF16).astype(F32)
    return (hi, mid, rest - mid)


def sincos_turns(u):
    f = u - jnp.round(u)
    q = f * f
    s = f * (SIN[0] + q * (SIN[1] + q * (SIN[2] + q * (SIN[3] + q * SIN[4]))))
    c = COS[0] + q * (COS[1] + q * (COS[2] + q * (COS[3] + q * COS[4])))
    s2 = s + s
    return s2 * c, 1.0 - s2 * s


def per_segment(rows):
    return jnp.concatenate([rows[k : k + 1] for k in range(K)], axis=1)


def one_hot_regions(region, count):
    return jnp.where(iota((count, region.shape[1]), 0).astype(F32) == region, 1.0, 0.0)


def scatter(onehot, slot, fields):
    n = fields.shape[0]
    total = None
    owner = (iota((PAD * n, slot.shape[1]), 0) // n).astype(F32) == slot
    for part in split3(fields):
        spread = jnp.where(owner, jnp.concatenate([part] * PAD, axis=0), 0.0).astype(BF16)
        piece = nt(onehot, spread)
        total = piece if total is None else total + piece
    return total


def pack_kernel(region_ref, count_ref, anchor_ref, direction_ref, length_ref, out_ref, slot_ref, column):
    region = per_segment(region_ref[...].astype(F32))
    live = count_ref[...].astype(F32)
    lengths = length_ref[...]
    blocks = []
    start = jnp.full((1, lengths.shape[1]), 0.5, F32)
    for k in range(K):
        length = lengths[k : k + 1]
        spacing = length / jnp.maximum(live[k : k + 1], 1.0)
        first = start + 0.5 * spacing
        points = anchor_ref[...] + first * direction_ref[...]
        steps = spacing * direction_ref[...]
        blocks.append(jnp.concatenate([points, steps, spacing, live[k : k + 1]], axis=0))
        start = start + length
    fields = jnp.concatenate(blocks, axis=1)
    segments = fields.shape[1]
    regions = out_ref.shape[0]
    key = (
        region * 32768.0
        + (fields[7:8] - 1.0) * 2048.0
        + iota((1, segments), 1).astype(F32)
    )
    for c in range(segments // LANES):
        chunk = key[:, c * LANES : (c + 1) * LANES]
        column[c * LANES : (c + 1) * LANES, :] = jnp.transpose(
            jnp.broadcast_to(chunk, (LANES, LANES))
        )
    onehot = one_hot_regions(region, regions)
    sizes = jnp.sum(onehot, axis=1, keepdims=True)
    above = jnp.sum(
        jnp.where(iota((regions, segments), 0).astype(F32) > region, sizes, 0.0),
        axis=0,
        keepdims=True,
    )
    larger = []
    for c in range(segments // LANES):
        chunk = key[:, c * LANES : (c + 1) * LANES]
        larger.append(
            jnp.sum(jnp.where(column[...] > chunk, 1.0, 0.0), axis=0, keepdims=True)
        )
    slot = jnp.concatenate(larger, axis=1) - above
    slot_ref[...] = slot
    out_ref[...] = scatter(onehot.astype(BF16), slot, fields)


def combine_kernel(region_ref, slot_ref, grad_ref, arrived_ref, colour_ref, out_ref):
    region = per_segment(region_ref[...].astype(F32))
    slot = slot_ref[...]
    regions = arrived_ref.shape[0]
    onehot = one_hot_regions(region, regions).astype(BF16)
    taken = None
    for part in split3(jnp.transpose(arrived_ref[...])):
        piece = nn(part.astype(BF16), onehot)
        taken = piece if taken is None else taken + piece
    rows = taken.shape[0]
    kept = jnp.where((iota(taken.shape, 0) // 4).astype(F32) == slot, taken, 0.0)
    total = kept[0:8]
    for r in range(8, rows, 8):
        total = total + kept[r : r + 8]
    values = total[0:4] + total[4:8]
    rays = grad_ref.shape[1]
    grad = grad_ref[...]
    seen = [jnp.ones((1, rays), F32)]
    colours = []
    for k in range(K):
        block = values[:, k * rays : (k + 1) * rays]
        colours.append(block[1:4])
        seen.append(seen[-1] * block[0:1])
    colour = seen[0] * colours[0]
    for k in range(1, K):
        colour = colour + seen[k] * colours[k]
    colour_ref[...] = colour
    behind = jnp.zeros((1, rays), F32)
    replies = [None] * K
    for k in reversed(range(K)):
        replies[k] = jnp.concatenate([grad * seen[k], behind], axis=0)
        pulled = grad * colours[k]
        behind = behind + seen[k] * (pulled[0:1] + pulled[1:2] + pulled[2:3])
    out_ref[...] = scatter(onehot, slot, jnp.concatenate(replies, axis=1))


def setup_kernel(freq_ref, w_ref, bias_ref, w_out_ref, turns_ref, wt_ref, bias_cols_ref, wot_ref, wo_ref):
    for c in range(3):
        turns_ref[c] = jnp.transpose(
            jnp.broadcast_to(freq_ref[c : c + 1, :] * TURN, (LANES, LANES))
        )
    wt_ref[...] = jnp.transpose(w_ref[...].astype(F32)).astype(BF16)
    for h in range(2):
        bias_cols_ref[h * LANES : (h + 1) * LANES, :] = jnp.transpose(
            jnp.broadcast_to(bias_ref[:, h * LANES : (h + 1) * LANES], (LANES, LANES))
        )
    padded = jnp.concatenate([w_out_ref[...].astype(F32), jnp.zeros((12, 256), F32)], axis=0)
    wo_ref[...] = padded.astype(BF16)
    wide = jnp.concatenate([padded, jnp.zeros((LANES - 16, 256), F32)], axis=0)
    wot_ref[...] = jnp.transpose(wide).astype(BF16)


def tile_fields(fields, p):
    two = fields[pl.ds(pl.multiple_of(p * 16, 16), 16), :]
    return jnp.concatenate([two[0:8], two[8:16]], axis=1)


def start_phases(x, turns_ref, even, odd, twice):
    lead, step = [], []
    for r in range(4):
        rows = slice(r * 32, (r + 1) * 32)
        wide = [jnp.concatenate([turns_ref[c, rows, :]] * 2, axis=1) for c in range(3)]
        lead = wide[0] * x[0:1] + wide[1] * x[1:2] + wide[2] * x[2:3]
        step = wide[0] * x[3:4] + wide[1] * x[4:5] + wide[2] * x[5:6]
        s0, c0 = sincos_turns(lead)
        sd, cd = sincos_turns(step)
        low = slice(LANES + r * 32, LANES + (r + 1) * 32)
        even[rows, :] = s0
        even[low, :] = c0
        odd[rows, :] = s0 * cd - c0 * sd
        odd[low, :] = c0 * cd + s0 * sd
        twice[rows, :] = cd + cd


def advance(this, last, twice):
    k = jnp.concatenate([twice[...]] * 2, axis=0)
    last[...] = k * this[...] - last[...]


def sigmoid(v):
    return 0.5 * jnp.tanh(0.5 * v) + 0.5


def softplus(v):
    return jnp.maximum(v, 0.0) + jnp.log1p(jnp.exp(-jnp.abs(v)))


def running_sum(x):
    row = iota(x.shape, 0)
    for shift in (1, 2, 4, 8):
        x = x + jnp.where(row >= shift, pltpu.roll(x, shift, 0), 0.0)
    return x


def absorbed(q):
    small = q * (1.0 - q * (0.5 - q * (1.0 / 6.0 - q * (1.0 / 24.0))))
    return jnp.where(q < 0.03, small, 1.0 - jnp.exp(-q))


def shade(raw, p, x, bias_ref):
    live = iota((S, 256), 0).astype(F32) < x[7:8]
    spacing = jnp.where(live, x[6:7], 0.0)
    outs = []
    for f in range(4):
        pair = [raw[2 * p + h, pl.ds(f, S, stride=8), :] for h in range(2)]
        outs.append(jnp.where(live, jnp.concatenate(pair, axis=1), 0.0) + bias_ref[0, f])
    sigma = softplus(outs[0])
    colours = [sigmoid(v) for v in outs[1:]]
    q = sigma * spacing
    through = running_sum(q)
    weight = jnp.exp(q - through) * absorbed(q)
    return outs[0], colours, spacing, through, weight


def forward_kernel(rec_ref, turns_ref, wt_ref, bias_ref, wo_ref, out_bias_ref, reply_ref, raw_ref, fields, even, odd, twice, reply):
    fields[...] = jnp.transpose(rec_ref[...])
    reply[...] = jnp.zeros_like(reply)
    tiles = SLOTS // 2
    bias = jnp.concatenate([bias_ref[...]] * 4, axis=1)

    def tile(p, _):
        x = tile_fields(fields, p)
        most = jnp.max(x[7:8]).astype(jnp.int32)
        start_phases(x, turns_ref, even, odd, twice)

        def step(i, _):
            first = even[...].astype(BF16)
            advance(even, odd, twice)
            second = odd[...].astype(BF16)
            advance(odd, even, twice)
            encoded = jnp.concatenate([first, second], axis=1)
            pre = nn(wt_ref[...], encoded) + bias
            hidden = (pre * sigmoid(pre)).astype(BF16)
            outs = nn(wo_ref[...], hidden)[0:8]
            both = jnp.concatenate([outs[:, 0:256], outs[:, 256:512]], axis=0)
            for h in range(2):
                raw_ref[2 * p + h, pl.ds(pl.multiple_of(i * 16, 16), 16), :] = both[
                    :, h * LANES : (h + 1) * LANES
                ]
            return 0

        lax.fori_loop(0, (most + 1) // 2, step, 0)
        _, colours, _, through, weight = shade(raw_ref, p, x, out_bias_ref)
        local = [jnp.exp(-through[S - 1 : S])] + [
            jnp.sum(weight * c, axis=0, keepdims=True) for c in colours
        ]
        block = jnp.concatenate(local, axis=0)
        reply[pl.ds(pl.multiple_of(p * 8, 8), 8), :] = jnp.concatenate(
            [block[:, 0:LANES], block[:, LANES:]], axis=0
        )
        return 0

    lax.fori_loop(0, tiles, tile, 0)
    reply_ref[...] = jnp.transpose(reply[...])


def middle_kernel(rec_ref, raw_ref, out_bias_ref, coef_ref, fields):
    fields[...] = jnp.transpose(rec_ref[...])

    def tile(p, _):
        x = tile_fields(fields, p)
        out0, colours, spacing, through, weight = shade(raw_ref, p, x, out_bias_ref)
        scale = spacing * sigmoid(out0)
        left = jnp.exp(-through)
        parts = []
        for c in colours:
            seen = running_sum(weight * c)
            later = seen[S - 1 : S] - seen
            parts.append(scale * (c * left - later))
        parts.append(-scale)
        for c in colours:
            parts.append(weight * c * (1.0 - c))
        coef_ref[p] = jnp.concatenate(parts, axis=0)
        return 0

    lax.fori_loop(0, SLOTS // 2, tile, 0)


def backward_kernel(rec_ref, ret_ref, turns_ref, wt_ref, bias_ref, wot_ref, coef_ref, gh_ref, gb_ref, go_ref, gob_ref, fields, pulls, even, odd, twice, pull_out, bias_sum, out_sum):
    fields[...] = jnp.transpose(rec_ref[...])
    pulls[...] = jnp.transpose(ret_ref[...])
    bias = jnp.concatenate([bias_ref[...]] * 4, axis=1)
    gh_ref[...] = jnp.zeros_like(gh_ref)
    go_ref[...] = jnp.zeros_like(go_ref)
    bias_sum[...] = jnp.zeros_like(bias_sum)
    out_sum[...] = jnp.zeros_like(out_sum)
    pull_out[...] = jnp.zeros_like(pull_out)

    def tile(p, _):
        x = tile_fields(fields, p)
        most = jnp.max(x[7:8]).astype(jnp.int32)
        start_phases(x, turns_ref, even, odd, twice)
        four = pulls[pl.ds(pl.multiple_of(p * 8, 8), 8), :]
        g = jnp.concatenate([four[0:4], four[4:8]], axis=1)
        coef = coef_ref[p]
        part = [coef[n * S : (n + 1) * S] for n in range(7)]
        outs = [part[0] * g[0:1] + part[1] * g[1:2] + part[2] * g[2:3] + part[3] * g[3:4]]
        outs += [part[4 + c] * g[c : c + 1] for c in range(3)]
        for f in range(4):
            out_sum[f * S : (f + 1) * S, :] += outs[f]
            for h in range(2):
                pull_out[h, pl.ds(f, S, stride=8), :] = outs[f][:, h * LANES : (h + 1) * LANES]

        def step(i, _):
            first = even[...].astype(BF16)
            advance(even, odd, twice)
            second = odd[...].astype(BF16)
            advance(odd, even, twice)
            encoded = jnp.concatenate([first, second], axis=1)
            pre = nn(wt_ref[...], encoded) + bias
            s = sigmoid(pre)
            h = pre * s
            hidden = h.astype(BF16)
            slope = s + h * (1.0 - s)
            rows = pl.ds(pl.multiple_of(i * 16, 16), 16)
            d = jnp.concatenate([pull_out[0, rows, :], pull_out[1, rows, :]], axis=1)
            d = jnp.concatenate([d[0:8], d[8:16]], axis=1)
            low = jnp.concatenate([d, jnp.zeros_like(d)], axis=0).astype(BF16)
            d_pre = nn(wot_ref[:, 0:16], low) * slope
            bias_sum[...] += (
                d_pre[:, 0:LANES]
                + d_pre[:, LANES : 2 * LANES]
                + d_pre[:, 2 * LANES : 3 * LANES]
                + d_pre[:, 3 * LANES :]
            )
            gh_ref[...] += nt(encoded, d_pre.astype(BF16))
            go_ref[...] += nt(low, hidden)[0:8]
            return 0

        lax.fori_loop(0, (most + 1) // 2, step, 0)
        return 0

    lax.fori_loop(0, SLOTS // 2, tile, 0)
    folded = jnp.transpose(bias_sum[...])
    gb_ref[...] = jnp.sum(folded, axis=0, keepdims=True)
    sums = [
        jnp.sum(out_sum[f * S : (f + 1) * S, :], axis=(0, 1), keepdims=True)
        for f in range(4)
    ]
    lane = iota((1, LANES), 1)
    row = jnp.zeros((1, LANES), F32)
    for f in range(4):
        row = jnp.where(lane == f, sums[f], row)
    gob_ref[...] = row


def sds(*shape, dtype=F32):
    return jax.ShapeDtypeStruct(shape, dtype)


def call(kernel, out_shape, scratch=(), in_specs=None, flops=0, transcendentals=0, touched=1 << 20):
    extra = {} if in_specs is None else {"in_specs": in_specs}
    return pl.pallas_call(
        kernel,
        out_shape=out_shape,
        **extra,
        scratch_shapes=list(scratch),
        compiler_params=pltpu.CompilerParams(vmem_limit_bytes=40 << 20),
        cost_estimate=pl.CostEstimate(
            flops=flops, bytes_accessed=touched, transcendentals=transcendentals
        ),
    )


VM = pl.BlockSpec(memory_space=pltpu.VMEM)
SM = pl.BlockSpec(memory_space=pltpu.SMEM)


def exchange(x):
    return lax.all_to_all(x, BOTH, split_axis=0, concat_axis=0, tiled=True)


def shards(anchors, directions, regions, counts, seg_len, color_grad, frequencies, w_hidden, b_hidden, w_out, b_out):
    count = lax.axis_size("rx") * lax.axis_size("ry")
    rays = regions.shape[0]
    region_rows = regions.T
    outbound, slot = call(
        pack_kernel,
        (sds(count, PAD * 8), sds(1, rays * K)),
        [pltpu.VMEM((rays * K, LANES), F32)],
    )(region_rows, counts.T, anchors, directions, seg_len)
    turns, w_t, bias_cols, wo_t, wo = call(
        setup_kernel,
        (
            sds(3, LANES, LANES),
            sds(256, 256, dtype=BF16),
            sds(256, LANES),
            sds(256, LANES, dtype=BF16),
            sds(16, 256, dtype=BF16),
        ),
    )(frequencies[0], w_hidden[0], b_hidden, w_out[0])
    received = exchange(outbound)
    tiles = SLOTS // 2
    phase_scratch = [
        pltpu.VMEM((256, 256), F32),
        pltpu.VMEM((256, 256), F32),
        pltpu.VMEM((LANES, 256), F32),
    ]
    reply, raw = call(
        forward_kernel,
        (sds(count, LANES), sds(SLOTS, 8 * S, LANES)),
        [pltpu.VMEM((PAD * 8, LANES), F32)] + phase_scratch + [pltpu.VMEM((LANES, LANES), F32)],
        in_specs=[VM] * 5 + [SM],
        flops=7 * 10**9,
    )(received, turns, w_t, bias_cols, wo, b_out)
    arrived = exchange(reply)
    coef = call(
        middle_kernel,
        sds(tiles, 7 * S, 256),
        [pltpu.VMEM((PAD * 8, LANES), F32)],
        in_specs=[VM, VM, SM],
    )(received, raw, b_out)
    colour, returning = call(
        combine_kernel,
        (sds(3, rays), sds(count, LANES)),
    )(region_rows, slot, color_grad, arrived)
    returned = exchange(returning)
    gh, gb, go, gob = call(
        backward_kernel,
        (sds(256, 256), sds(1, 256), sds(8, 256), sds(1, LANES)),
        [pltpu.VMEM((PAD * 8, LANES), F32), pltpu.VMEM((LANES, LANES), F32)]
        + phase_scratch
        + [
            pltpu.VMEM((2, 8 * S, LANES), F32),
            pltpu.VMEM((256, LANES), F32),
            pltpu.VMEM((4 * S, 256), F32),
        ],
        flops=20 * 10**9,
    )(received, returned, turns, w_t, bias_cols, wo_t, coef)
    return (colour, gh[None], gb, go[None, 0:4], gob[:, 0:4])


def solution(mesh):
    spread = P(BOTH)
    in_specs = (
        P(None, BOTH),
        P(None, BOTH),
        spread,
        spread,
        P(None, BOTH),
        P(None, BOTH),
        spread,
        spread,
        spread,
        spread,
        spread,
    )
    out_specs = (P(None, BOTH), spread, spread, spread, spread)
    return jax.shard_map(
        shards, mesh=mesh, in_specs=in_specs, out_specs=out_specs, check_vma=False
    )
```

```python
import functools

import jax
import jax.numpy as jnp
from jax import lax
from jax.experimental import pallas as pl
from jax.experimental.pallas import tpu as pltpu
from jax.sharding import PartitionSpec as P

S = 16
K = 4
SLOTS = 24
PAD = 32
TILES = SLOTS // 2
GROUPS = SLOTS // 4
LANES = 128
BOTH = ("rx", "ry")
F32 = jnp.float32
BF16 = jnp.bfloat16
SIN = (3.14159264, -5.16771009, 2.55007766, -0.59829216, 0.07765941)
COS = (0.99999995, -4.93479286, 4.05841191, -1.33188016, 0.21969679)
TURN = 0.15915494309189535


def iota(shape, axis):
    return lax.broadcasted_iota(jnp.int32, shape, axis)


def nt(a, b):
    return lax.dot_general(a, b, (((1,), (1,)), ((), ())), preferred_element_type=F32)


def nn(a, b):
    return lax.dot_general(a, b, (((1,), (0,)), ((), ())), preferred_element_type=F32)


def split3(x):
    hi = x.astype(BF16).astype(F32)
    rest = x - hi
    mid = rest.astype(BF16).astype(F32)
    return (hi, mid, rest - mid)


def sincos_turns(u):
    f = u - jnp.round(u)
    q = f * f
    s = f * (SIN[0] + q * (SIN[1] + q * (SIN[2] + q * (SIN[3] + q * SIN[4]))))
    c = COS[0] + q * (COS[1] + q * (COS[2] + q * (COS[3] + q * COS[4])))
    s2 = s + s
    return s2 * c, 1.0 - s2 * s


def per_segment(rows):
    return jnp.concatenate([rows[k : k + 1] for k in range(K)], axis=1)


def one_hot_regions(region, count):
    return jnp.where(iota((count, region.shape[1]), 0).astype(F32) == region, 1.0, 0.0)


def scatter(onehot, slot, fields):
    n = fields.shape[0]
    total = None
    owner = (iota((PAD * n, slot.shape[1]), 0) // n).astype(F32) == slot
    for part in split3(fields):
        spread = jnp.where(owner, jnp.concatenate([part] * PAD, axis=0), 0.0).astype(BF16)
        piece = nt(onehot, spread)
        total = piece if total is None else total + piece
    return total


def pack_kernel(region_ref, count_ref, anchor_ref, direction_ref, length_ref, out_ref, slot_ref, column):
    region = per_segment(region_ref[...].astype(F32))
    live = count_ref[...].astype(F32)
    lengths = length_ref[...]
    blocks = []
    start = jnp.full((1, lengths.shape[1]), 0.5, F32)
    for k in range(K):
        length = lengths[k : k + 1]
        spacing = length / jnp.maximum(live[k : k + 1], 1.0)
        first = start + 0.5 * spacing
        points = anchor_ref[...] + first * direction_ref[...]
        steps = spacing * direction_ref[...]
        blocks.append(jnp.concatenate([points, steps, spacing, live[k : k + 1]], axis=0))
        start = start + length
    fields = jnp.concatenate(blocks, axis=1)
    segments = fields.shape[1]
    regions = out_ref.shape[0]
    key = (
        region * 32768.0
        + (fields[7:8] - 1.0) * 2048.0
        + iota((1, segments), 1).astype(F32)
    )
    for c in range(segments // LANES):
        chunk = key[:, c * LANES : (c + 1) * LANES]
        column[c * LANES : (c + 1) * LANES, :] = jnp.transpose(
            jnp.broadcast_to(chunk, (LANES, LANES))
        )
    onehot = one_hot_regions(region, regions)
    sizes = jnp.sum(onehot, axis=1, keepdims=True)
    above = jnp.sum(
        jnp.where(iota((regions, segments), 0).astype(F32) > region, sizes, 0.0),
        axis=0,
        keepdims=True,
    )
    larger = []
    for c in range(segments // LANES):
        chunk = key[:, c * LANES : (c + 1) * LANES]
        larger.append(
            jnp.sum(jnp.where(column[...] > chunk, 1.0, 0.0), axis=0, keepdims=True)
        )
    slot = jnp.concatenate(larger, axis=1) - above
    slot_ref[...] = slot
    out_ref[...] = scatter(onehot.astype(BF16), slot, fields)


def combine_kernel(region_ref, slot_ref, grad_ref, arrived_ref, colour_ref, out_ref):
    region = per_segment(region_ref[...].astype(F32))
    slot = slot_ref[...]
    regions = arrived_ref.shape[0]
    onehot = one_hot_regions(region, regions).astype(BF16)
    taken = None
    for part in split3(jnp.transpose(arrived_ref[...])):
        piece = nn(part.astype(BF16), onehot)
        taken = piece if taken is None else taken + piece
    rows = taken.shape[0]
    kept = jnp.where((iota(taken.shape, 0) // 4).astype(F32) == slot, taken, 0.0)
    total = kept[0:8]
    for r in range(8, rows, 8):
        total = total + kept[r : r + 8]
    values = total[0:4] + total[4:8]
    rays = grad_ref.shape[1]
    grad = grad_ref[...]
    seen = [jnp.ones((1, rays), F32)]
    colours = []
    for k in range(K):
        block = values[:, k * rays : (k + 1) * rays]
        colours.append(block[1:4])
        seen.append(seen[-1] * block[0:1])
    colour = seen[0] * colours[0]
    for k in range(1, K):
        colour = colour + seen[k] * colours[k]
    colour_ref[...] = colour
    behind = jnp.zeros((1, rays), F32)
    replies = [None] * K
    for k in reversed(range(K)):
        replies[k] = jnp.concatenate([grad * seen[k], behind], axis=0)
        pulled = grad * colours[k]
        behind = behind + seen[k] * (pulled[0:1] + pulled[1:2] + pulled[2:3])
    out_ref[...] = scatter(onehot, slot, jnp.concatenate(replies, axis=1))


def setup_kernel(freq_ref, w_ref, bias_ref, w_out_ref, turns_ref, wt_ref, bias_cols_ref, wot_ref, wo_ref):
    for c in range(3):
        turns_ref[c] = jnp.transpose(
            jnp.broadcast_to(freq_ref[c : c + 1, :] * TURN, (LANES, LANES))
        )
    wt_ref[...] = (0.5 * jnp.transpose(w_ref[...].astype(F32))).astype(BF16)
    for h in range(2):
        bias_cols_ref[h * LANES : (h + 1) * LANES, :] = jnp.transpose(
            0.5 * jnp.broadcast_to(bias_ref[:, h * LANES : (h + 1) * LANES], (LANES, LANES))
        )
    padded = jnp.concatenate([w_out_ref[...].astype(F32), jnp.zeros((12, 256), F32)], axis=0)
    wo_ref[...] = padded.astype(BF16)
    wide = jnp.concatenate([padded, jnp.zeros((LANES - 16, 256), F32)], axis=0)
    wot_ref[...] = (0.5 * jnp.transpose(wide)).astype(BF16)


def tile_fields(fields, p):
    two = fields[pl.ds(pl.multiple_of(p * 16, 16), 16), :]
    return jnp.concatenate([two[0:8], two[8:16]], axis=1)


def start_phases(fields, q, turns_ref, even, odd, twice):
    for h in range(4):
        x = fields[pl.ds(pl.multiple_of(q * 32 + h * 8, 8), 8), :]
        lanes = slice(h * LANES, (h + 1) * LANES)
        for r in range(4):
            rows = slice(r * 32, (r + 1) * 32)
            turns = [turns_ref[c, rows, :] for c in range(3)]
            s0, c0 = sincos_turns(turns[0] * x[0:1] + turns[1] * x[1:2] + turns[2] * x[2:3])
            sd, cd = sincos_turns(turns[0] * x[3:4] + turns[1] * x[4:5] + turns[2] * x[5:6])
            low = slice(LANES + r * 32, LANES + (r + 1) * 32)
            even[rows, lanes] = s0
            even[low, lanes] = c0
            odd[rows, lanes] = s0 * cd - c0 * sd
            odd[low, lanes] = c0 * cd + s0 * sd
            twice[rows, lanes] = cd + cd


def encode_pair(even, odd, twice, encoded, quarters=range(4)):
    for r in quarters:
        rows = slice(r * 32, (r + 1) * 32)
        for h in range(4):
            lanes = slice(h * LANES, (h + 1) * LANES)
            k = twice[rows, lanes]
            for part in (rows, slice(LANES + r * 32, LANES + (r + 1) * 32)):
                now, last = even[part, lanes], odd[part, lanes]
                following = k * now - last
                even[part, lanes] = k * following - now
                odd[part, lanes] = following
                encoded[part, lanes] = now.astype(BF16)
                encoded[part, 512 + h * LANES : 512 + (h + 1) * LANES] = following.astype(BF16)


def count_pairs(fields, halves):
    total = jnp.int32(0)
    for q in range(GROUPS):
        most = [fields[q * 32 + h * 8 + 7 : q * 32 + h * 8 + 8, :] for h in range(4)]
        most = jnp.maximum(jnp.maximum(most[0], most[1]), jnp.maximum(most[2], most[3]))
        half = (jnp.max(most).astype(jnp.int32) + 1) // 2
        halves[q] = half
        total = total + half
    return total


def walk(start, run, halves, total):
    turns = (total + 3) // 2
    nowhere = (jnp.int32(GROUPS), jnp.int32(0))

    def body(turn, carry):
        q, i, before, older = carry
        for parity in range(2):
            valid = 2 * turn + parity < total
            now = (jnp.where(valid, q, GROUPS), jnp.where(valid, i, 0))

            fresh = jnp.logical_and(valid, i == 0).astype(jnp.int32)
            lax.fori_loop(0, fresh, functools.partial(start, q), 0)
            more = i + 1 < halves[jnp.minimum(q, GROUPS - 1)]
            q = jnp.where(more, q, q + 1)
            i = jnp.where(more, i + 1, 0)
            run(before, older, parity)
            before, older = now, before
        return (q, i, before, older)

    lax.fori_loop(0, turns, body, (jnp.int32(0), jnp.int32(0), nowhere, nowhere))


def sigmoid(v):
    return 0.5 * jnp.tanh(0.5 * v) + 0.5


def softplus(v):
    return jnp.maximum(v, 0.0) + jnp.log1p(jnp.exp(-jnp.abs(v)))


def running_sum(x):
    row = iota(x.shape, 0)
    for shift in (1, 2, 4, 8):
        x = x + jnp.where(row >= shift, pltpu.roll(x, shift, 0), 0.0)
    return x


def absorbed(q):
    small = q * (1.0 - q * (0.5 - q * (1.0 / 6.0 - q * (1.0 / 24.0))))
    return jnp.where(q < 0.03, small, 1.0 - jnp.exp(-q))


def shade(raw, p, x, bias_ref):
    live = iota((S, 256), 0).astype(F32) < x[7:8]
    spacing = jnp.where(live, x[6:7], 0.0)
    outs = []
    for f in range(4):
        pair = [raw[2 * p + h, pl.ds(f, S, stride=8), :] for h in range(2)]
        outs.append(jnp.where(live, jnp.concatenate(pair, axis=1), 0.0) + bias_ref[0, f])
    sigma = softplus(outs[0])
    colours = [sigmoid(v) for v in outs[1:]]
    q = sigma * spacing
    through = running_sum(q)
    weight = jnp.exp(q - through) * absorbed(q)
    return outs[0], colours, spacing, through, weight


def forward_kernel(rec_ref, turns_ref, wt_ref, bias_ref, wo_ref, out_bias_ref, reply_ref, raw_ref, fields, even, odd, twice, encoded0, encoded1, hidden0, hidden1, halves, reply):
    fields[...] = jnp.transpose(rec_ref[...])
    reply[...] = jnp.zeros_like(reply)
    for zeroed in (encoded0, encoded1, hidden0, hidden1):
        zeroed[...] = jnp.zeros_like(zeroed)

    total = count_pairs(fields, halves)
    encoded, hidden = (encoded0, encoded1), (hidden0, hidden1)

    def start(q, _, unused):
        start_phases(fields, q, turns_ref, even, odd, twice)
        return 0

    def run(before, older, parity):
        other = 1 - parity
        bias = jnp.concatenate([bias_ref[...]] * 2, axis=1)
        wt = wt_ref[...]
        chunks = [slice(n * 256, (n + 1) * 256) for n in range(4)]

        def activate(n, v):
            hidden[other][:, chunks[n]] = (v * jnp.tanh(v) + v).astype(BF16)

        def layer(n):
            return nn(wt, encoded[other][:, chunks[n]]) + bias

        q, i = older
        rows = pl.ds(pl.multiple_of(i * 16, 16), 16)
        outs = []
        v = layer(0)
        encode_pair(even, odd, twice, encoded[parity], [0])
        for n in range(4):
            following = layer(n + 1) if n < 3 else None
            activate(n, v)
            if n < 3:
                encode_pair(even, odd, twice, encoded[parity], [n + 1])
            v = following
        wide = nn(wo_ref[...], hidden[parity][...])[0:8]
        outs = [wide[:, c] for c in chunks]
        for h in range(4):
            lanes = slice(h % 2 * LANES, (h % 2 + 1) * LANES)
            raw_ref[4 * q + h, rows, :] = jnp.concatenate(
                [outs[h // 2][:, lanes], outs[2 + h // 2][:, lanes]], axis=0
            )

    walk(start, run, halves, total)

    def finish(p, _):
        x = tile_fields(fields, p)
        _, colours, _, through, weight = shade(raw_ref, p, x, out_bias_ref)
        local = [jnp.exp(-through[S - 1 : S])] + [
            jnp.sum(weight * c, axis=0, keepdims=True) for c in colours
        ]
        block = jnp.concatenate(local, axis=0)
        reply[pl.ds(pl.multiple_of(p * 8, 8), 8), :] = jnp.concatenate(
            [block[:, 0:LANES], block[:, LANES:]], axis=0
        )
        return 0

    lax.fori_loop(0, TILES, finish, 0)
    reply_ref[...] = jnp.transpose(reply[...])


def middle_kernel(rec_ref, raw_ref, out_bias_ref, coef_ref, fields):
    fields[...] = jnp.transpose(rec_ref[...])

    def tile(p, _):
        x = tile_fields(fields, p)
        out0, colours, spacing, through, weight = shade(raw_ref, p, x, out_bias_ref)
        scale = spacing * sigmoid(out0)
        left = jnp.exp(-through)
        parts = []
        for c in colours:
            seen = running_sum(weight * c)
            later = seen[S - 1 : S] - seen
            parts.append(scale * (c * left - later))
        parts.append(-scale)
        for c in colours:
            parts.append(weight * c * (1.0 - c))
        coef_ref[p] = jnp.concatenate(parts, axis=0)
        return 0

    lax.fori_loop(0, SLOTS // 2, tile, 0)


def backward_kernel(rec_ref, ret_ref, turns_ref, wt_ref, bias_ref, wot_ref, coef_ref, gh_ref, gb_ref, go_ref, gob_ref, fields, pulls, even, odd, twice, encoded0, encoded1, hidden0, copied0, d_hidden0, d_low0, hidden1, copied1, d_hidden1, d_low1, halves, pull_out, bias_sum, out_sum):
    fields[...] = jnp.transpose(rec_ref[...])
    pulls[...] = jnp.transpose(ret_ref[...])
    for zeroed in (gh_ref, go_ref, bias_sum, out_sum, encoded0, encoded1, hidden0, copied0, d_hidden0, d_low0, hidden1, copied1, d_hidden1, d_low1):
        zeroed[...] = jnp.zeros_like(zeroed)
    pull_out[SLOTS:] = jnp.zeros((4, 8 * S, LANES), F32)

    def prepare(p, _):
        four = pulls[pl.ds(pl.multiple_of(p * 8, 8), 8), :]
        g = jnp.concatenate([four[0:4], four[4:8]], axis=1)
        coef = coef_ref[p]
        part = [coef[n * S : (n + 1) * S] for n in range(7)]
        outs = [part[0] * g[0:1] + part[1] * g[1:2] + part[2] * g[2:3] + part[3] * g[3:4]]
        outs += [part[4 + c] * g[c : c + 1] for c in range(3)]
        zeros = jnp.zeros((S, LANES), F32)
        for f in range(4):
            out_sum[f * S : (f + 1) * S, :] += outs[f]
            for h in range(2):
                pull_out[2 * p + h, pl.ds(f, S, stride=8), :] = outs[f][:, h * LANES : (h + 1) * LANES]
                pull_out[2 * p + h, pl.ds(f + 4, S, stride=8), :] = zeros
        return 0

    lax.fori_loop(0, TILES, prepare, 0)
    total = count_pairs(fields, halves)

    encoded = (encoded0, encoded1)
    products = ((hidden0, copied0, d_hidden0, d_low0), (hidden1, copied1, d_hidden1, d_low1))

    def start(q, _, unused):
        start_phases(fields, q, turns_ref, even, odd, twice)
        return 0

    def run(before, older, parity):
        other = 1 - parity
        hidden1, copied1, d_hidden1, d_low1 = products[parity]
        hidden, copied, d_hidden, d_low = products[other]
        bias = jnp.concatenate([bias_ref[...]] * 2, axis=1)
        wt = wt_ref[...]
        wot = wot_ref[:, 0:16]
        q, i = before
        rows = pl.ds(pl.multiple_of(i * 16, 16), 16)
        four = [pull_out[4 * q + h, rows, :] for h in range(4)]
        chunks = [slice(n * 256, (n + 1) * 256) for n in range(4)]

        def layer(n):
            d = jnp.concatenate(four[n % 2 * 2 : n % 2 * 2 + 2], axis=1)
            d = d[n // 2 * 8 : n // 2 * 8 + 8]
            low = jnp.concatenate([d, jnp.zeros_like(d)], axis=0).astype(BF16)
            enc = encoded[other][:, chunks[n]]
            copied[:, chunks[n]] = enc
            d_low[:, chunks[n]] = low
            return nn(wt, enc) + bias, nn(wot, low)

        def activate(n, v, d):
            t = jnp.tanh(v)
            u = t + 1.0
            h = v * u
            slope = u + h * (1.0 - t)
            d_pre = d * slope
            d_hidden[:, chunks[n]] = d_pre.astype(BF16)
            hidden[:, chunks[n]] = h.astype(BF16)
            return d_pre[:, 0:LANES] + d_pre[:, LANES:]

        summed = bias_sum[...]
        v = layer(0)
        encode_pair(even, odd, twice, encoded[parity], [0])
        for n in range(4):
            following = layer(n + 1) if n < 3 else None
            if n == 0:
                gh_ref[...] += nt(copied1[...], d_hidden1[...])
            summed = summed + activate(n, *v)
            if n < 3:
                encode_pair(even, odd, twice, encoded[parity], [n + 1])
            if n == 2:
                go_ref[...] += nt(d_low1[...], hidden1[...])[0:8]
            v = following
        bias_sum[...] = summed

    walk(start, run, halves, total)
    folded = jnp.transpose(bias_sum[...])
    gb_ref[...] = jnp.sum(folded, axis=0, keepdims=True)
    sums = [
        jnp.sum(out_sum[f * S : (f + 1) * S, :], axis=(0, 1), keepdims=True)
        for f in range(4)
    ]
    lane = iota((1, LANES), 1)
    row = jnp.zeros((1, LANES), F32)
    for f in range(4):
        row = jnp.where(lane == f, sums[f], row)
    gob_ref[...] = row


def sds(*shape, dtype=F32):
    return jax.ShapeDtypeStruct(shape, dtype)


def call(kernel, out_shape, scratch=(), in_specs=None, flops=0, transcendentals=0, touched=1 << 20):
    extra = {} if in_specs is None else {"in_specs": in_specs}
    return pl.pallas_call(
        kernel,
        out_shape=out_shape,
        **extra,
        scratch_shapes=list(scratch),
        compiler_params=pltpu.CompilerParams(vmem_limit_bytes=40 << 20),
        cost_estimate=pl.CostEstimate(
            flops=flops, bytes_accessed=touched, transcendentals=transcendentals
        ),
    )


VM = pl.BlockSpec(memory_space=pltpu.VMEM)
SM = pl.BlockSpec(memory_space=pltpu.SMEM)


def phase_scratch():
    return [
        pltpu.VMEM((256, 512), F32),
        pltpu.VMEM((256, 512), F32),
        pltpu.VMEM((LANES, 512), F32),
    ]


def region_forward(received, turns, w_t, bias_cols, wo, b_out):
    wide = pltpu.VMEM((256, 1024), BF16)
    return call(
        forward_kernel,
        (sds(received.shape[0], LANES), sds(SLOTS + 4, 8 * S, LANES)),
        [pltpu.VMEM((PAD * 8, LANES), F32)]
        + phase_scratch()
        + [wide] * 4 + [pltpu.SMEM((GROUPS,), jnp.int32), pltpu.VMEM((LANES, LANES), F32)],
        in_specs=[VM] * 5 + [SM],
        flops=7 * 10**9,
    )(received, turns, w_t, bias_cols, wo, b_out)


def region_middle(received, raw, b_out):
    return call(
        middle_kernel,
        sds(TILES, 7 * S, 256),
        [pltpu.VMEM((PAD * 8, LANES), F32)],
        in_specs=[VM, VM, SM],
    )(received, raw, b_out)


def region_backward(received, returned, turns, w_t, bias_cols, wo_t, coef):
    wide = pltpu.VMEM((256, 1024), BF16)
    return call(
        backward_kernel,
        (sds(256, 256), sds(1, 256), sds(8, 256), sds(1, LANES)),
        [pltpu.VMEM((PAD * 8, LANES), F32), pltpu.VMEM((LANES, LANES), F32)]
        + phase_scratch()
        + [
            wide,
            wide,
        ]
        + [wide, wide, wide, pltpu.VMEM((16, 1024), BF16)] * 2
        + [
            pltpu.SMEM((GROUPS,), jnp.int32),
            pltpu.VMEM((SLOTS + 4, 8 * S, LANES), F32),
            pltpu.VMEM((256, LANES), F32),
            pltpu.VMEM((4 * S, 256), F32),
        ],
        flops=20 * 10**9,
    )(received, returned, turns, w_t, bias_cols, wo_t, coef)


def exchange(x):
    return lax.all_to_all(x, BOTH, split_axis=0, concat_axis=0, tiled=True)


def shards(anchors, directions, regions, counts, seg_len, color_grad, frequencies, w_hidden, b_hidden, w_out, b_out):
    count = lax.axis_size("rx") * lax.axis_size("ry")
    rays = regions.shape[0]
    region_rows = regions.T
    outbound, slot = call(
        pack_kernel,
        (sds(count, PAD * 8), sds(1, rays * K)),
        [pltpu.VMEM((rays * K, LANES), F32)],
    )(region_rows, counts.T, anchors, directions, seg_len)
    turns, w_t, bias_cols, wo_t, wo = call(
        setup_kernel,
        (
            sds(3, LANES, LANES),
            sds(256, 256, dtype=BF16),
            sds(256, LANES),
            sds(256, LANES, dtype=BF16),
            sds(16, 256, dtype=BF16),
        ),
    )(frequencies[0], w_hidden[0], b_hidden, w_out[0])
    received = exchange(outbound)
    reply, raw = region_forward(received, turns, w_t, bias_cols, wo, b_out)
    arrived = exchange(reply)
    coef = region_middle(received, raw, b_out)
    colour, returning = call(
        combine_kernel,
        (sds(3, rays), sds(count, LANES)),
    )(region_rows, slot, color_grad, arrived)
    returned = exchange(returning)
    gh, gb, go, gob = region_backward(received, returned, turns, w_t, bias_cols, wo_t, coef)
    return (colour, gh[None], gb, go[None, 0:4], gob[:, 0:4])


def solution(mesh):
    spread = P(BOTH)
    in_specs = (
        P(None, BOTH),
        P(None, BOTH),
        spread,
        spread,
        P(None, BOTH),
        P(None, BOTH),
        spread,
        spread,
        spread,
        spread,
        spread,
    )
    out_specs = (P(None, BOTH), spread, spread, spread, spread)
    return jax.shard_map(
        shards, mesh=mesh, in_specs=in_specs, out_specs=out_specs, check_vma=False
    )
```

```python
import functools

import jax
import jax.numpy as jnp
from jax import lax
from jax.experimental import pallas as pl
from jax.experimental.pallas import tpu as pltpu
from jax.sharding import PartitionSpec as P

S = 16
K = 4
SLOTS = 24
PAD = 32
TILES = SLOTS // 2
GROUPS = SLOTS // 4
STEPS = GROUPS * S // 2
RING_OUT = 8
RING_IN = 16
LANES = 128
BOTH = ("rx", "ry")
F32 = jnp.float32
BF16 = jnp.bfloat16
SIN = (3.14159264, -5.16771009, 2.55007766, -0.59829216, 0.07765941)
COS = (0.99999995, -4.93479286, 4.05841191, -1.33188016, 0.21969679)
TURN = 0.15915494309189535


def iota(shape, axis):
    return lax.broadcasted_iota(jnp.int32, shape, axis)


def nt(a, b):
    return lax.dot_general(a, b, (((1,), (1,)), ((), ())), preferred_element_type=F32)


def nn(a, b):
    return lax.dot_general(a, b, (((1,), (0,)), ((), ())), preferred_element_type=F32)


def split3(x):
    hi = x.astype(BF16).astype(F32)
    rest = x - hi
    mid = rest.astype(BF16).astype(F32)
    return (hi, mid, rest - mid)


def sincos_turns(u):
    f = u - jnp.round(u)
    q = f * f
    s = f * (SIN[0] + q * (SIN[1] + q * (SIN[2] + q * (SIN[3] + q * SIN[4]))))
    c = COS[0] + q * (COS[1] + q * (COS[2] + q * (COS[3] + q * COS[4])))
    s2 = s + s
    return s2 * c, 1.0 - s2 * s


def per_segment(rows):
    return jnp.concatenate([rows[k : k + 1] for k in range(K)], axis=1)


def one_hot_regions(region, count):
    return jnp.where(iota((count, region.shape[1]), 0).astype(F32) == region, 1.0, 0.0)


def scatter(onehot, slot, fields):
    n = fields.shape[0]
    total = None
    owner = (iota((PAD * n, slot.shape[1]), 0) // n).astype(F32) == slot
    for part in split3(fields):
        spread = jnp.where(owner, jnp.concatenate([part] * PAD, axis=0), 0.0).astype(BF16)
        piece = nt(onehot, spread)
        total = piece if total is None else total + piece
    return total


def pack_kernel(region_in, count_in, anchor_in, direction_in, length_in, out_ref, slot_ref, column, region_ref, count_ref, anchor_ref, direction_ref, length_ref, sems):
    sources = (region_in, count_in, anchor_in, direction_in, length_in)
    places = (region_ref, count_ref, anchor_ref, direction_ref, length_ref)
    copies = [
        pltpu.make_async_copy(source, place, sems.at[n])
        for n, (source, place) in enumerate(zip(sources, places))
    ]
    for copy in copies:
        copy.start()
    for copy in copies:
        copy.wait()
    region = per_segment(region_ref[...].astype(F32))
    live = count_ref[...].astype(F32)
    lengths = length_ref[...]
    blocks = []
    start = jnp.full((1, lengths.shape[1]), 0.5, F32)
    for k in range(K):
        length = lengths[k : k + 1]
        spacing = length / jnp.maximum(live[k : k + 1], 1.0)
        first = start + 0.5 * spacing
        points = anchor_ref[...] + first * direction_ref[...]
        steps = spacing * direction_ref[...]
        blocks.append(jnp.concatenate([points, steps, spacing, live[k : k + 1]], axis=0))
        start = start + length
    fields = jnp.concatenate(blocks, axis=1)
    segments = fields.shape[1]
    regions = out_ref.shape[0] // 2
    key = (
        region * 32768.0
        + (fields[7:8] - 1.0) * 2048.0
        + iota((1, segments), 1).astype(F32)
    )
    for c in range(segments // LANES):
        chunk = key[:, c * LANES : (c + 1) * LANES]
        column[c * LANES : (c + 1) * LANES, :] = jnp.transpose(
            jnp.broadcast_to(chunk, (LANES, LANES))
        )
    onehot = one_hot_regions(region, regions)
    sizes = jnp.sum(onehot, axis=1, keepdims=True)
    above = jnp.sum(
        jnp.where(iota((regions, segments), 0).astype(F32) > region, sizes, 0.0),
        axis=0,
        keepdims=True,
    )
    larger = []
    for c in range(segments // LANES):
        chunk = key[:, c * LANES : (c + 1) * LANES]
        larger.append(
            jnp.sum(jnp.where(column[...] > chunk, 1.0, 0.0), axis=0, keepdims=True)
        )
    slot = jnp.concatenate(larger, axis=1) - above
    slot_ref[...] = slot
    packed = scatter(onehot.astype(BF16), slot, fields)
    for h in range(2):
        out_ref[pl.ds(h, regions, stride=2), :] = packed[:, h * LANES : (h + 1) * LANES]


def unpack(rec_ref, fields):
    for h in range(2):
        rows = rec_ref[pl.ds(h, rec_ref.shape[0] // 2, stride=2), :]
        fields[h * LANES : (h + 1) * LANES, :] = jnp.transpose(rows)


def combine_kernel(region_ref, slot_ref, grad_ref, arrived_ref, colour_ref, out_ref):
    region = per_segment(region_ref[...].astype(F32))
    slot = slot_ref[...]
    regions = arrived_ref.shape[0]
    onehot = one_hot_regions(region, regions).astype(BF16)
    taken = None
    for part in split3(jnp.transpose(arrived_ref[...])):
        piece = nn(part.astype(BF16), onehot)
        taken = piece if taken is None else taken + piece
    rows = taken.shape[0]
    kept = jnp.where((iota(taken.shape, 0) // 4).astype(F32) == slot, taken, 0.0)
    total = kept[0:8]
    for r in range(8, rows, 8):
        total = total + kept[r : r + 8]
    values = total[0:4] + total[4:8]
    rays = grad_ref.shape[1]
    grad = grad_ref[...]
    seen = [jnp.ones((1, rays), F32)]
    colours = []
    for k in range(K):
        block = values[:, k * rays : (k + 1) * rays]
        colours.append(block[1:4])
        seen.append(seen[-1] * block[0:1])
    colour = seen[0] * colours[0]
    for k in range(1, K):
        colour = colour + seen[k] * colours[k]
    colour_ref[...] = colour
    behind = jnp.zeros((1, rays), F32)
    replies = [None] * K
    for k in reversed(range(K)):
        replies[k] = jnp.concatenate([grad * seen[k], behind], axis=0)
        pulled = grad * colours[k]
        behind = behind + seen[k] * (pulled[0:1] + pulled[1:2] + pulled[2:3])
    out_ref[...] = scatter(onehot, slot, jnp.concatenate(replies, axis=1))


def setup_kernel(freq_ref, w_ref, bias_ref, w_out_ref, turns_ref, wt_ref, bias_cols_ref, wot_ref, wo_ref):
    for c in range(3):
        turns_ref[c] = jnp.transpose(
            jnp.broadcast_to(freq_ref[c : c + 1, :] * TURN, (LANES, LANES))
        )
    wt_ref[...] = (0.5 * jnp.transpose(w_ref[...].astype(F32))).astype(BF16)
    for h in range(2):
        bias_cols_ref[h * LANES : (h + 1) * LANES, :] = jnp.transpose(
            0.5 * jnp.broadcast_to(bias_ref[:, h * LANES : (h + 1) * LANES], (LANES, LANES))
        )
    padded = jnp.concatenate([w_out_ref[...].astype(F32), jnp.zeros((12, 256), F32)], axis=0)
    wo_ref[...] = padded.astype(BF16)
    wide = jnp.concatenate([padded, jnp.zeros((LANES - 16, 256), F32)], axis=0)
    wot_ref[...] = (0.5 * jnp.transpose(wide)).astype(BF16)


def tile_fields(fields, p):
    two = fields[pl.ds(pl.multiple_of(p * 16, 16), 16), :]
    return jnp.concatenate([two[0:8], two[8:16]], axis=1)


def start_phases(fields, q, turns_ref, even, odd, twice):
    for h in range(4):
        x = fields[pl.ds(pl.multiple_of(q * 32 + h * 8, 8), 8), :]
        lanes = slice(h * LANES, (h + 1) * LANES)
        for r in range(4):
            rows = slice(r * 32, (r + 1) * 32)
            turns = [turns_ref[c, rows, :] for c in range(3)]
            s0, c0 = sincos_turns(turns[0] * x[0:1] + turns[1] * x[1:2] + turns[2] * x[2:3])
            sd, cd = sincos_turns(turns[0] * x[3:4] + turns[1] * x[4:5] + turns[2] * x[5:6])
            low = slice(LANES + r * 32, LANES + (r + 1) * 32)
            even[rows, lanes] = s0
            even[low, lanes] = c0
            odd[rows, lanes] = s0 * cd - c0 * sd
            odd[low, lanes] = c0 * cd + s0 * sd
            twice[rows, lanes] = cd + cd


def encode_pair(even, odd, twice, encoded, quarters=range(4)):
    for r in quarters:
        rows = slice(r * 32, (r + 1) * 32)
        for h in range(4):
            lanes = slice(h * LANES, (h + 1) * LANES)
            k = twice[rows, lanes]
            for part in (rows, slice(LANES + r * 32, LANES + (r + 1) * 32)):
                now, last = even[part, lanes], odd[part, lanes]
                following = k * now - last
                even[part, lanes] = k * following - now
                odd[part, lanes] = following
                encoded[part, lanes] = now.astype(BF16)
                encoded[part, 512 + h * LANES : 512 + (h + 1) * LANES] = following.astype(BF16)


def count_pairs(fields, halves):
    total = jnp.int32(0)
    for q in range(GROUPS):
        most = [fields[q * 32 + h * 8 + 7 : q * 32 + h * 8 + 8, :] for h in range(4)]
        most = jnp.maximum(jnp.maximum(most[0], most[1]), jnp.maximum(most[2], most[3]))
        half = (jnp.max(most).astype(jnp.int32) + 1) // 2
        halves[q] = half
        total = total + half
    return total


def walk(start, halves, total, turns, run):
    nowhere = (jnp.int32(GROUPS), jnp.int32(0))

    def body(turn, carry):
        q, i, before, older = carry
        for parity in range(2):
            valid = 2 * turn + parity < total
            now = (jnp.where(valid, q, GROUPS), jnp.where(valid, i, 0))

            if start is not None:
                fresh = jnp.logical_and(valid, i == 0).astype(jnp.int32)
                lax.fori_loop(0, fresh, functools.partial(start, q), 0)
            more = i + 1 < halves[jnp.minimum(q, GROUPS - 1)]
            q = jnp.where(more, q, q + 1)
            i = jnp.where(more, i + 1, 0)
            run(2 * turn + parity, now, before, older, parity)
            before, older = now, before
        return (q, i, before, older)

    carry = (jnp.int32(0), jnp.int32(0), nowhere, nowhere)
    lax.fori_loop(0, turns, body, carry)


def sigmoid(v):
    return 0.5 * jnp.tanh(0.5 * v) + 0.5


def softplus(v):
    return jnp.maximum(v, 0.0) + jnp.log1p(jnp.exp(-jnp.abs(v)))


def running_sum(x):
    row = iota(x.shape, 0)
    for shift in (1, 2, 4, 8):
        x = x + jnp.where(row >= shift, pltpu.roll(x, shift, 0), 0.0)
    return x


def absorbed(q):
    small = q * (1.0 - q * (0.5 - q * (1.0 / 6.0 - q * (1.0 / 24.0))))
    return jnp.where(q < 0.03, small, 1.0 - jnp.exp(-q))


def shade(raw, p, x, bias_ref):
    live = iota((S, 256), 0).astype(F32) < x[7:8]
    spacing = jnp.where(live, x[6:7], 0.0)
    outs = []
    for f in range(4):
        pair = [raw[2 * p + h, pl.ds(f, S, stride=8), :] for h in range(2)]
        outs.append(jnp.where(live, jnp.concatenate(pair, axis=1), 0.0) + bias_ref[0, f])
    sigma = softplus(outs[0])
    colours = [sigmoid(v) for v in outs[1:]]
    q = sigma * spacing
    through = running_sum(q)
    weight = jnp.exp(q - through) * absorbed(q)
    return outs[0], colours, spacing, through, weight


def forward_kernel(rec_ref, turns_ref, wt_ref, bias_ref, wo_ref, out_bias_ref, reply_ref, raw_ref, encoded_ref, layer_ref, fields, even, odd, twice, hidden0, hidden1, encoded, layer, halves, reply, sems):
    unpack(rec_ref, fields)
    reply[...] = jnp.zeros_like(reply)
    for zeroed in (hidden0, hidden1):
        zeroed[...] = jnp.zeros_like(zeroed)

    total = count_pairs(fields, halves)
    hidden = (hidden0, hidden1)

    def copy(which, n):
        held, kept = ((encoded, encoded_ref), (layer, layer_ref))[which]
        slot = lax.rem(n, RING_OUT)
        return pltpu.make_async_copy(held.at[slot], kept.at[n], sems.at[which, slot])

    def keep(due, which, n, begin):
        @pl.when(due)
        def _():
            if begin:
                copy(which, n).start()
            else:
                copy(which, n).wait()

    def start(q, _, unused):
        start_phases(fields, q, turns_ref, even, odd, twice)
        return 0

    def run(t, now, before, older, parity):
        other = 1 - parity
        fresh = encoded.at[lax.rem(t, RING_OUT)]
        place = lax.rem(t + RING_OUT - 1, RING_OUT)
        keep(t >= RING_OUT, 0, t - RING_OUT, False)
        keep(t > RING_OUT, 1, t - 1 - RING_OUT, False)
        keep(t >= 1, 0, t - 1, True)
        keep(t >= 2, 1, t - 2, True)
        bias = jnp.concatenate([bias_ref[...]] * 2, axis=1)
        wt = wt_ref[...]
        chunks = [slice(n * 256, (n + 1) * 256) for n in range(4)]

        def activate(n, v):
            hidden[other][:, chunks[n]] = (v * jnp.tanh(v) + v).astype(BF16)
            layer[place, :, chunks[n]] = v.astype(BF16)

        def worked(n):
            return nn(wt, encoded[place, :, chunks[n]]) + bias

        q, i = older
        rows = pl.ds(pl.multiple_of(i * 16, 16), 16)
        outs = []
        v = worked(0)
        encode_pair(even, odd, twice, fresh, [0])
        for n in range(4):
            following = worked(n + 1) if n < 3 else None
            activate(n, v)
            if n < 3:
                encode_pair(even, odd, twice, fresh, [n + 1])
            v = following
        wide = nn(wo_ref[...], hidden[parity][...])[0:8]
        outs = [wide[:, c] for c in chunks]
        for h in range(4):
            lanes = slice(h % 2 * LANES, (h % 2 + 1) * LANES)
            raw_ref[4 * q + h, rows, :] = jnp.concatenate(
                [outs[h // 2][:, lanes], outs[2 + h // 2][:, lanes]], axis=0
            )

    turns = (total + 3) // 2
    walk(start, halves, total, turns, run)
    steps = 2 * turns

    def drain(which, n, _):
        copy(which, n).wait()
        return 0

    lax.fori_loop(jnp.maximum(steps - RING_OUT, 0), steps - 1, functools.partial(drain, 0), 0)
    lax.fori_loop(jnp.maximum(steps - 1 - RING_OUT, 0), steps - 2, functools.partial(drain, 1), 0)

    def finish(p, _):
        x = tile_fields(fields, p)
        _, colours, _, through, weight = shade(raw_ref, p, x, out_bias_ref)
        local = [jnp.exp(-through[S - 1 : S])] + [
            jnp.sum(weight * c, axis=0, keepdims=True) for c in colours
        ]
        block = jnp.concatenate(local, axis=0)
        reply[pl.ds(pl.multiple_of(p * 8, 8), 8), :] = jnp.concatenate(
            [block[:, 0:LANES], block[:, LANES:]], axis=0
        )
        return 0

    lax.fori_loop(0, TILES, finish, 0)
    reply_ref[...] = jnp.transpose(reply[...])


def middle_kernel(rec_ref, raw_ref, out_bias_ref, coef_ref, fields):
    unpack(rec_ref, fields)

    def tile(p, _):
        x = tile_fields(fields, p)
        out0, colours, spacing, through, weight = shade(raw_ref, p, x, out_bias_ref)
        scale = spacing * sigmoid(out0)
        left = jnp.exp(-through)
        parts = []
        for c in colours:
            seen = running_sum(weight * c)
            later = seen[S - 1 : S] - seen
            parts.append(scale * (c * left - later))
        parts.append(-scale)
        for c in colours:
            parts.append(weight * c * (1.0 - c))
        coef_ref[p] = jnp.concatenate(parts, axis=0)
        return 0

    lax.fori_loop(0, SLOTS // 2, tile, 0)


def backward_kernel(rec_ref, ret_ref, wot_ref, coef_ref, encoded_ref, layer_ref, gh_ref, gb_ref, go_ref, gob_ref, fields, pulls, hidden0, d_hidden0, d_low0, hidden1, d_hidden1, d_low1, halves, pull_out, bias_sum, go_sum, out_sum, encoded, layer, sems):
    unpack(rec_ref, fields)
    pulls[...] = jnp.transpose(ret_ref[...])
    total = count_pairs(fields, halves)

    def copies(n):
        slot = lax.rem(n, RING_IN)
        return (
            pltpu.make_async_copy(encoded_ref.at[n], encoded.at[slot], sems.at[0, slot]),
            pltpu.make_async_copy(layer_ref.at[n], layer.at[slot], sems.at[1, slot]),
        )

    def fetch(n, _):
        for copy in copies(n):
            copy.start()
        return 0

    lax.fori_loop(0, jnp.minimum(RING_IN - 2, total), fetch, 0)
    for zeroed in (gh_ref, go_sum, bias_sum, out_sum, hidden1, d_hidden1, d_low1):
        zeroed[...] = jnp.zeros_like(zeroed)
    pull_out[SLOTS:] = jnp.zeros((4, 8 * S, LANES), F32)

    def prepare(p, _):
        four = pulls[pl.ds(pl.multiple_of(p * 8, 8), 8), :]
        g = jnp.concatenate([four[0:4], four[4:8]], axis=1)
        coef = coef_ref[p]
        part = [coef[n * S : (n + 1) * S] for n in range(7)]
        outs = [part[0] * g[0:1] + part[1] * g[1:2] + part[2] * g[2:3] + part[3] * g[3:4]]
        outs += [part[4 + c] * g[c : c + 1] for c in range(3)]
        zeros = jnp.zeros((S, LANES), F32)
        for f in range(4):
            out_sum[f * S : (f + 1) * S, :] += outs[f]
            for h in range(2):
                pull_out[2 * p + h, pl.ds(f, S, stride=8), :] = outs[f][:, h * LANES : (h + 1) * LANES]
                pull_out[2 * p + h, pl.ds(f + 4, S, stride=8), :] = zeros
        return 0

    lax.fori_loop(0, TILES, prepare, 0)

    products = ((hidden0, d_hidden0, d_low0), (hidden1, d_hidden1, d_low1))

    def run(t, now, before, older, parity):
        @pl.when(t < total)
        def _():
            for copy in copies(t):
                copy.wait()

        @pl.when(t + RING_IN - 2 < total)
        def _():
            for copy in copies(t + RING_IN - 2):
                copy.start()

        place = lax.rem(jnp.minimum(t, total - 1), RING_IN)
        earlier = lax.rem(jnp.maximum(jnp.minimum(t - 1, total - 1), 0), RING_IN)
        hidden1, d_hidden1, d_low1 = products[1 - parity]
        hidden, d_hidden, d_low = products[parity]
        wot = wot_ref[:, 0:16]
        q, i = now
        rows = pl.ds(pl.multiple_of(i * 16, 16), 16)
        four = [pull_out[4 * q + h, rows, :] for h in range(4)]
        chunks = [slice(n * 256, (n + 1) * 256) for n in range(4)]

        def pulled(n):
            d = jnp.concatenate(four[n % 2 * 2 : n % 2 * 2 + 2], axis=1)
            d = d[n // 2 * 8 : n // 2 * 8 + 8]
            low = jnp.concatenate([d, jnp.zeros_like(d)], axis=0).astype(BF16)
            d_low[:, chunks[n]] = low
            return nn(wot, low)

        def activate(n, d):
            v = layer[place, :, chunks[n]].astype(F32)
            t = jnp.tanh(v)
            u = t + 1.0
            h = v * u
            slope = u + h * (1.0 - t)
            d_pre = d * slope
            d_hidden[:, chunks[n]] = d_pre.astype(BF16)
            hidden[:, chunks[n]] = h.astype(BF16)
            return d_pre[:, 0:LANES] + d_pre[:, LANES:]

        summed = bias_sum[...]
        d = pulled(0)
        for n in range(4):
            following = pulled(n + 1) if n < 3 else None
            gh_ref[...] += nt(encoded[earlier, :, chunks[n]], d_hidden1[:, chunks[n]])
            summed = summed + activate(n, d)
            go_sum[...] += nt(d_low1[:, chunks[n]], hidden1[:, chunks[n]])[0:8]
            d = following
        bias_sum[...] = summed

    turns = jnp.where(total > 0, (total + 2) // 2, 0)
    walk(None, halves, total, turns, run)
    go_ref[...] = go_sum[0:4]
    folded = jnp.transpose(bias_sum[...])
    gb_ref[...] = jnp.sum(folded, axis=0, keepdims=True)
    sums = [
        jnp.sum(out_sum[f * S : (f + 1) * S, :], axis=(0, 1), keepdims=True)
        for f in range(4)
    ]
    lane = iota((1, 4), 1)
    row = jnp.zeros((1, 4), F32)
    for f in range(4):
        row = jnp.where(lane == f, sums[f], row)
    gob_ref[...] = row


def sds(*shape, dtype=F32):
    return jax.ShapeDtypeStruct(shape, dtype)


def call(kernel, out_shape, scratch=(), in_specs=None, flops=0, transcendentals=0, touched=1 << 20, vmem=6.0, out_specs=None):
    extra = {} if in_specs is None else {"in_specs": in_specs}
    if out_specs is not None:
        extra["out_specs"] = out_specs
    return pl.pallas_call(
        kernel,
        out_shape=out_shape,
        **extra,
        scratch_shapes=list(scratch),
        compiler_params=pltpu.CompilerParams(vmem_limit_bytes=int(vmem * (1 << 20))),
        cost_estimate=pl.CostEstimate(
            flops=flops, bytes_accessed=touched, transcendentals=transcendentals
        ),
    )


VM = pl.BlockSpec(memory_space=pltpu.VMEM)
SM = pl.BlockSpec(memory_space=pltpu.SMEM)
HBM = pl.BlockSpec(memory_space=pl.ANY)
FAR = pl.BlockSpec(memory_space=pltpu.HBM)


def phase_scratch():
    return [
        pltpu.VMEM((256, 512), F32),
        pltpu.VMEM((256, 512), F32),
        pltpu.VMEM((LANES, 512), F32),
    ]


def region_forward(received, turns, w_t, bias_cols, wo, b_out):
    wide = pltpu.VMEM((256, 1024), BF16)
    return call(
        forward_kernel,
        (
            sds(received.shape[0] // 2, LANES),
            sds(SLOTS + 4, 8 * S, LANES),
            sds(STEPS + 2, 256, 1024, dtype=BF16),
            sds(STEPS + 2, 256, 1024, dtype=BF16),
        ),
        [pltpu.VMEM((PAD * 8, LANES), F32)]
        + phase_scratch()
        + [wide] * 2
        + [pltpu.VMEM((RING_OUT, 256, 1024), BF16)] * 2
        + [
            pltpu.SMEM((GROUPS,), jnp.int32),
            pltpu.VMEM((LANES, LANES), F32),
            pltpu.SemaphoreType.DMA((2, RING_OUT)),
        ],
        out_specs=(VM, VM, FAR, FAR),
        in_specs=[VM] * 5 + [SM],
        flops=7 * 10**9,
        vmem=44.0,
    )(received, turns, w_t, bias_cols, wo, b_out)


def region_middle(received, raw, b_out):
    return call(
        middle_kernel,
        sds(TILES, 7 * S, 256),
        [pltpu.VMEM((PAD * 8, LANES), F32)],
        in_specs=[VM, VM, SM],
        vmem=4.0,
    )(received, raw, b_out)


def region_backward(received, returned, wo_t, coef, encoded, layer):
    wide = pltpu.VMEM((256, 1024), BF16)
    return call(
        backward_kernel,
        (sds(256, 256), sds(1, 256), sds(4, 256), sds(1, 4)),
        [pltpu.VMEM((PAD * 8, LANES), F32), pltpu.VMEM((LANES, LANES), F32)]
        + [wide, wide, pltpu.VMEM((16, 1024), BF16)] * 2
        + [
            pltpu.SMEM((GROUPS,), jnp.int32),
            pltpu.VMEM((SLOTS + 4, 8 * S, LANES), F32),
            pltpu.VMEM((256, LANES), F32),
            pltpu.VMEM((8, 256), F32),
            pltpu.VMEM((4 * S, 256), F32),
            pltpu.VMEM((RING_IN, 256, 1024), BF16),
            pltpu.VMEM((RING_IN, 256, 1024), BF16),
            pltpu.SemaphoreType.DMA((2, RING_IN)),
        ],
        in_specs=[VM] * 4 + [HBM] * 2,
        flops=20 * 10**9,
        vmem=44.0,
    )(received, returned, wo_t, coef, encoded, layer)


def exchange(x):
    return lax.all_to_all(x, BOTH, split_axis=0, concat_axis=0, tiled=True)


def shards(anchors, directions, regions, counts, seg_len, color_grad, frequencies, w_hidden, b_hidden, w_out, b_out):
    count = lax.axis_size("rx") * lax.axis_size("ry")
    rays = regions.shape[0]
    region_rows = regions.T
    outbound, slot = call(
        pack_kernel,
        (sds(count * 2, LANES), sds(1, rays * K)),
        [
            pltpu.VMEM((rays * K, LANES), F32),
            pltpu.VMEM((K, rays), jnp.int32),
            pltpu.VMEM((K, rays), jnp.int32),
            pltpu.VMEM((3, rays), F32),
            pltpu.VMEM((3, rays), F32),
            pltpu.VMEM((K, rays), F32),
            pltpu.SemaphoreType.DMA((5,)),
        ],
        in_specs=[FAR] * 5,
        vmem=60.0,
    )(region_rows, counts.T, anchors, directions, seg_len)
    turns, w_t, bias_cols, wo_t, wo = call(
        setup_kernel,
        (
            sds(3, LANES, LANES),
            sds(256, 256, dtype=BF16),
            sds(256, LANES),
            sds(256, LANES, dtype=BF16),
            sds(16, 256, dtype=BF16),
        ),
    )(frequencies[0], w_hidden[0], b_hidden, w_out[0])
    received = exchange(outbound)
    reply, raw, encoded, layer = region_forward(received, turns, w_t, bias_cols, wo, b_out)
    arrived = exchange(reply)
    coef = region_middle(received, raw, b_out)
    colour, returning = call(
        combine_kernel,
        (sds(3, rays), sds(count, LANES)),
        vmem=5.0,
    )(region_rows, slot, color_grad, arrived)
    returned = exchange(returning)
    gh, gb, go, gob = region_backward(received, returned, wo_t, coef, encoded, layer)
    return (colour, gh[None], gb, go[None], gob)


def solution(mesh):
    spread = P(BOTH)
    in_specs = (
        P(None, BOTH),
        P(None, BOTH),
        spread,
        spread,
        P(None, BOTH),
        P(None, BOTH),
        spread,
        spread,
        spread,
        spread,
        spread,
    )
    out_specs = (P(None, BOTH), spread, spread, spread, spread)
    return jax.shard_map(
        shards, mesh=mesh, in_specs=in_specs, out_specs=out_specs, check_vma=False
    )
```

```python
import functools

import jax
import jax.numpy as jnp
from jax import lax
from jax.experimental import pallas as pl
from jax.experimental.pallas import tpu as pltpu
from jax.sharding import PartitionSpec as P

S = 16
K = 4
SLOTS = 24
PAD = 32
TILES = SLOTS // 2
GROUPS = SLOTS // 4
STEPS = GROUPS * S // 2
RING_OUT = 8
RING_IN = 16
LANES = 128
BOTH = ("rx", "ry")
F32 = jnp.float32
BF16 = jnp.bfloat16
SIN = (3.14159264, -5.16771009, 2.55007766, -0.59829216, 0.07765941)
COS = (0.99999995, -4.93479286, 4.05841191, -1.33188016, 0.21969679)
TURN = 0.15915494309189535


def iota(shape, axis):
    return lax.broadcasted_iota(jnp.int32, shape, axis)


def nt(a, b):
    return lax.dot_general(a, b, (((1,), (1,)), ((), ())), preferred_element_type=F32)


def nn(a, b):
    return lax.dot_general(a, b, (((1,), (0,)), ((), ())), preferred_element_type=F32)


def split3(x):
    hi = x.astype(BF16).astype(F32)
    rest = x - hi
    mid = rest.astype(BF16).astype(F32)
    return (hi, mid, rest - mid)


def split2(x):
    return split3(x)[0:2]


def sincos_turns(u):
    f = u - jnp.round(u)
    q = f * f
    s = f * (SIN[0] + q * (SIN[1] + q * (SIN[2] + q * (SIN[3] + q * SIN[4]))))
    c = COS[0] + q * (COS[1] + q * (COS[2] + q * (COS[3] + q * COS[4])))
    s2 = s + s
    return s2 * c, 1.0 - s2 * s


def per_segment(rows):
    return jnp.concatenate([rows[k : k + 1] for k in range(K)], axis=1)


def one_hot_regions(region, count):
    return jnp.where(iota((count, region.shape[1]), 0).astype(F32) == region, 1.0, 0.0)


def scatter(onehot, slot, fields, split):
    n = fields.shape[0]
    total = None
    owner = (iota((SLOTS * n, slot.shape[1]), 0) // n).astype(F32) == slot
    rest = jnp.zeros(((PAD - SLOTS) * n, slot.shape[1]), BF16)
    for part in split(fields):
        spread = jnp.where(owner, jnp.concatenate([part] * SLOTS, axis=0), 0.0).astype(BF16)
        piece = nt(onehot, jnp.concatenate([spread, rest], axis=0))
        total = piece if total is None else total + piece
    return total


def pack_kernel(region_in, count_in, anchor_in, direction_in, length_in, out_ref, slot_ref, column, region_ref, count_ref, anchor_ref, direction_ref, length_ref, sems):
    sources = (region_in, count_in, anchor_in, direction_in, length_in)
    places = (region_ref, count_ref, anchor_ref, direction_ref, length_ref)
    copies = [
        pltpu.make_async_copy(source, place, sems.at[n])
        for n, (source, place) in enumerate(zip(sources, places))
    ]
    for copy in copies:
        copy.start()
    for copy in copies:
        copy.wait()
    region = per_segment(region_ref[...].astype(F32))
    live = count_ref[...].astype(F32)
    lengths = length_ref[...]
    blocks = []
    start = jnp.full((1, lengths.shape[1]), 0.5, F32)
    for k in range(K):
        length = lengths[k : k + 1]
        spacing = length / jnp.maximum(live[k : k + 1], 1.0)
        first = start + 0.5 * spacing
        points = anchor_ref[...] + first * direction_ref[...]
        steps = spacing * direction_ref[...]
        blocks.append(jnp.concatenate([points, steps, spacing, live[k : k + 1]], axis=0))
        start = start + length
    fields = jnp.concatenate(blocks, axis=1)
    segments = fields.shape[1]
    regions = out_ref.shape[0] // 2
    key = (
        region * 32768.0
        + (fields[7:8] - 1.0) * 2048.0
        + iota((1, segments), 1).astype(F32)
    )
    for c in range(segments // LANES):
        chunk = key[:, c * LANES : (c + 1) * LANES]
        column[c * LANES : (c + 1) * LANES, :] = jnp.transpose(
            jnp.broadcast_to(chunk, (LANES, LANES))
        )
    onehot = one_hot_regions(region, regions)
    sizes = jnp.sum(onehot, axis=1, keepdims=True)
    above = jnp.sum(
        jnp.where(iota((regions, segments), 0).astype(F32) > region, sizes, 0.0),
        axis=0,
        keepdims=True,
    )
    larger = []
    for c in range(segments // LANES):
        chunk = key[:, c * LANES : (c + 1) * LANES]
        larger.append(
            jnp.sum(jnp.where(column[...] > chunk, 1.0, 0.0), axis=0, keepdims=True)
        )
    slot = jnp.concatenate(larger, axis=1) - above
    slot_ref[...] = slot
    packed = scatter(onehot.astype(BF16), slot, fields, split3)
    for h in range(2):
        out_ref[pl.ds(h, regions, stride=2), :] = packed[:, h * LANES : (h + 1) * LANES]


def unpack(rec_ref, fields):
    for h in range(2):
        rows = rec_ref[pl.ds(h, rec_ref.shape[0] // 2, stride=2), :]
        fields[h * LANES : (h + 1) * LANES, :] = jnp.transpose(rows)


def combine_kernel(region_ref, slot_ref, grad_ref, arrived_ref, colour_ref, out_ref):
    region = per_segment(region_ref[...].astype(F32))
    slot = slot_ref[...]
    regions = arrived_ref.shape[0]
    onehot = one_hot_regions(region, regions).astype(BF16)
    taken = None
    for part in split2(jnp.transpose(arrived_ref[...])[0 : SLOTS * 4]):
        piece = nn(part.astype(BF16), onehot)
        taken = piece if taken is None else taken + piece
    rows = taken.shape[0]
    kept = jnp.where((iota(taken.shape, 0) // 4).astype(F32) == slot, taken, 0.0)
    total = kept[0:8]
    for r in range(8, rows, 8):
        total = total + kept[r : r + 8]
    values = total[0:4] + total[4:8]
    rays = grad_ref.shape[1]
    grad = grad_ref[...]
    seen = [jnp.ones((1, rays), F32)]
    colours = []
    for k in range(K):
        block = values[:, k * rays : (k + 1) * rays]
        colours.append(block[1:4])
        seen.append(seen[-1] * block[0:1])
    colour = seen[0] * colours[0]
    for k in range(1, K):
        colour = colour + seen[k] * colours[k]
    colour_ref[...] = colour
    behind = jnp.zeros((1, rays), F32)
    replies = [None] * K
    for k in reversed(range(K)):
        replies[k] = jnp.concatenate([grad * seen[k], behind], axis=0)
        pulled = grad * colours[k]
        behind = behind + seen[k] * (pulled[0:1] + pulled[1:2] + pulled[2:3])
    out_ref[...] = scatter(onehot, slot, jnp.concatenate(replies, axis=1), split2)


def setup_kernel(freq_ref, w_ref, bias_ref, w_out_ref, out_bias_ref, turns_ref, wt_ref, bias_cols_ref, wot_ref, wo_ref, out_rows_ref):
    b = out_bias_ref[...]
    rows = [jnp.broadcast_to(b[:, f : f + 1], (1, 256)) for f in range(4)]
    out_rows_ref[...] = jnp.concatenate(rows + rows, axis=0)
    for c in range(3):
        turns_ref[c] = jnp.transpose(
            jnp.broadcast_to(freq_ref[c : c + 1, :] * TURN, (LANES, LANES))
        )
    wt_ref[...] = (0.5 * jnp.transpose(w_ref[...].astype(F32))).astype(BF16)
    for h in range(2):
        bias_cols_ref[h * LANES : (h + 1) * LANES, :] = jnp.transpose(
            0.5 * jnp.broadcast_to(bias_ref[:, h * LANES : (h + 1) * LANES], (LANES, LANES))
        )
    padded = jnp.concatenate([w_out_ref[...].astype(F32), jnp.zeros((12, 256), F32)], axis=0)
    wo_ref[...] = padded.astype(BF16)
    wide = jnp.concatenate([padded, jnp.zeros((LANES - 16, 256), F32)], axis=0)
    wot_ref[...] = (0.5 * jnp.transpose(wide)).astype(BF16)


def tile_fields(fields, p):
    two = fields[pl.ds(pl.multiple_of(p * 16, 16), 16), :]
    return jnp.concatenate([two[0:8], two[8:16]], axis=1)


def start_phases(fields, q, turns_ref, even, odd, twice):
    for h in range(4):
        x = fields[pl.ds(pl.multiple_of(q * 32 + h * 8, 8), 8), :]
        lanes = slice(h * LANES, (h + 1) * LANES)
        for r in range(4):
            rows = slice(r * 32, (r + 1) * 32)
            turns = [turns_ref[c, rows, :] for c in range(3)]
            s0, c0 = sincos_turns(turns[0] * x[0:1] + turns[1] * x[1:2] + turns[2] * x[2:3])
            sd, cd = sincos_turns(turns[0] * x[3:4] + turns[1] * x[4:5] + turns[2] * x[5:6])
            low = slice(LANES + r * 32, LANES + (r + 1) * 32)
            even[rows, lanes] = s0
            even[low, lanes] = c0
            odd[rows, lanes] = s0 * cd - c0 * sd
            odd[low, lanes] = c0 * cd + s0 * sd
            twice[rows, lanes] = cd + cd


def encode_pair(even, odd, twice, encoded, quarters=range(4)):
    for r in quarters:
        rows = slice(r * 32, (r + 1) * 32)
        for h in range(4):
            lanes = slice(h * LANES, (h + 1) * LANES)
            k = twice[rows, lanes]
            for part in (rows, slice(LANES + r * 32, LANES + (r + 1) * 32)):
                now, last = even[part, lanes], odd[part, lanes]
                following = k * now - last
                even[part, lanes] = k * following - now
                odd[part, lanes] = following
                encoded[part, lanes] = now.astype(BF16)
                encoded[part, 512 + h * LANES : 512 + (h + 1) * LANES] = following.astype(BF16)


def count_pairs(fields, halves):
    total = jnp.int32(0)
    for q in range(GROUPS):
        most = [fields[q * 32 + h * 8 + 7 : q * 32 + h * 8 + 8, :] for h in range(4)]
        most = jnp.maximum(jnp.maximum(most[0], most[1]), jnp.maximum(most[2], most[3]))
        half = (jnp.max(most).astype(jnp.int32) + 1) // 2
        halves[q] = half
        total = total + half
    return total


def walk(start, halves, total, turns, run):
    nowhere = (jnp.int32(GROUPS), jnp.int32(0))

    def body(turn, carry):
        q, i, before, older = carry
        for parity in range(2):
            valid = 2 * turn + parity < total
            now = (jnp.where(valid, q, GROUPS), jnp.where(valid, i, 0))

            if start is not None:
                fresh = jnp.logical_and(valid, i == 0).astype(jnp.int32)
                lax.fori_loop(0, fresh, functools.partial(start, q), 0)
            more = i + 1 < halves[jnp.minimum(q, GROUPS - 1)]
            q = jnp.where(more, q, q + 1)
            i = jnp.where(more, i + 1, 0)
            run(2 * turn + parity, now, before, older, parity)
            before, older = now, before
        return (q, i, before, older)

    carry = (jnp.int32(0), jnp.int32(0), nowhere, nowhere)
    lax.fori_loop(0, turns, body, carry)


def sigmoid(v):
    return 0.5 * jnp.tanh(0.5 * v) + 0.5


def softplus(v):
    return jnp.maximum(v, 0.0) + jnp.log1p(jnp.exp(-jnp.abs(v)))


def running_sum(x):
    row = iota(x.shape, 0)
    for shift in (1, 2, 4, 8):
        x = x + jnp.where(row >= shift, pltpu.roll(x, shift, 0), 0.0)
    return x


def absorbed(q):
    small = q * (1.0 - q * (0.5 - q * (1.0 / 6.0 - q * (1.0 / 24.0))))
    return jnp.where(q < 0.03, small, 1.0 - jnp.exp(-q))


def shade(raw, p, x, bias_ref):
    live = iota((S, 256), 0).astype(F32) < x[7:8]
    spacing = jnp.where(live, x[6:7], 0.0)
    outs = []
    for f in range(4):
        pair = [raw[2 * p + h, pl.ds(f, S, stride=8), :] for h in range(2)]
        outs.append(jnp.where(live, jnp.concatenate(pair, axis=1), 0.0) + bias_ref[f : f + 1, :])
    sigma = softplus(outs[0])
    colours = [sigmoid(v) for v in outs[1:]]
    q = sigma * spacing
    through = running_sum(q)
    weight = jnp.exp(q - through) * absorbed(q)
    return outs[0], colours, spacing, through, weight


def forward_kernel(rec_ref, turns_ref, wt_ref, bias_ref, wo_ref, out_bias_ref, reply_ref, raw_ref, encoded_ref, layer_ref, fields, even, odd, twice, hidden0, hidden1, encoded0, encoded1, layer, halves, reply, sems):
    unpack(rec_ref, fields)
    reply[...] = jnp.zeros_like(reply)
    for zeroed in (hidden0, hidden1):
        zeroed[...] = jnp.zeros_like(zeroed)

    total = count_pairs(fields, halves)
    hidden = (hidden0, hidden1)

    encoded = (encoded0, encoded1)

    def copy(which, n, parity):
        slot = lax.rem(n, RING_OUT)
        held = layer.at[slot] if which else encoded[parity].at[lax.div(slot, 2)]
        kept = layer_ref if which else encoded_ref
        return pltpu.make_async_copy(held, kept.at[n], sems.at[which, slot])

    def keep(due, which, n, begin, parity):
        @pl.when(due)
        def _():
            if begin:
                copy(which, n, parity).start()
            else:
                copy(which, n, parity).wait()

    def start(q, _, unused):
        start_phases(fields, q, turns_ref, even, odd, twice)
        return 0

    def run(t, now, before, older, parity):
        other = 1 - parity
        fresh = encoded[parity].at[lax.div(lax.rem(t, RING_OUT), 2)]
        place = lax.rem(t + RING_OUT - 1, RING_OUT)
        behind = lax.div(place, 2)
        keep(t >= RING_OUT, 0, t - RING_OUT, False, parity)
        keep(t > RING_OUT, 1, t - 1 - RING_OUT, False, other)
        keep(t >= 1, 0, t - 1, True, other)
        keep(t >= 2, 1, t - 2, True, parity)
        bias = jnp.concatenate([bias_ref[...]] * 2, axis=1)
        wt = wt_ref[...]
        chunks = [slice(n * 256, (n + 1) * 256) for n in range(4)]

        def activate(n, v):
            hidden[other][:, chunks[n]] = (v * jnp.tanh(v) + v).astype(BF16)
            layer[place, :, chunks[n]] = v.astype(BF16)

        def worked(n):
            return nn(wt, encoded[other][behind, :, chunks[n]]) + bias

        q, i = older
        rows = pl.ds(pl.multiple_of(i * 16, 16), 16)
        outs = []
        v = worked(0)
        encode_pair(even, odd, twice, fresh, [0])
        for n in range(4):
            following = worked(n + 1) if n < 3 else None
            activate(n, v)
            if n < 3:
                encode_pair(even, odd, twice, fresh, [n + 1])
            v = following
        wide = nn(wo_ref[...], hidden[parity][...])[0:8]
        outs = [wide[:, c] for c in chunks]
        for h in range(4):
            lanes = slice(h % 2 * LANES, (h % 2 + 1) * LANES)
            raw_ref[4 * q + h, rows, :] = jnp.concatenate(
                [outs[h // 2][:, lanes], outs[2 + h // 2][:, lanes]], axis=0
            )

    turns = (total + 3) // 2
    walk(start, halves, total, turns, run)
    steps = 2 * turns

    def drain(which, n, _):
        for parity in range(2):
            keep(lax.rem(n, 2) == parity, which, n, False, parity)
        return 0

    lax.fori_loop(jnp.maximum(steps - RING_OUT, 0), steps - 1, functools.partial(drain, 0), 0)
    lax.fori_loop(jnp.maximum(steps - 1 - RING_OUT, 0), steps - 2, functools.partial(drain, 1), 0)

    def finish(p, _):
        x = tile_fields(fields, p)
        _, colours, _, through, weight = shade(raw_ref, p, x, out_bias_ref)
        local = [jnp.exp(-through[S - 1 : S])] + [
            jnp.sum(weight * c, axis=0, keepdims=True) for c in colours
        ]
        block = jnp.concatenate(local, axis=0)
        reply[pl.ds(pl.multiple_of(p * 8, 8), 8), :] = jnp.concatenate(
            [block[:, 0:LANES], block[:, LANES:]], axis=0
        )
        return 0

    lax.fori_loop(0, TILES, finish, 0)
    reply_ref[...] = jnp.transpose(reply[...])


def middle_kernel(rec_ref, raw_ref, out_bias_ref, coef_ref, fields):
    unpack(rec_ref, fields)

    def tile(p, _):
        x = tile_fields(fields, p)
        out0, colours, spacing, through, weight = shade(raw_ref, p, x, out_bias_ref)
        scale = spacing * sigmoid(out0)
        left = jnp.exp(-through)
        parts = []
        for c in colours:
            seen = running_sum(weight * c)
            later = seen[S - 1 : S] - seen
            parts.append(scale * (c * left - later))
        parts.append(-scale)
        for c in colours:
            parts.append(weight * c * (1.0 - c))
        coef_ref[p] = jnp.concatenate(parts, axis=0)
        return 0

    lax.fori_loop(0, SLOTS // 2, tile, 0)


def backward_kernel(rec_ref, ret_ref, wot_ref, coef_ref, encoded_ref, layer_ref, gh_ref, gb_ref, go_ref, gob_ref, fields, pulls, hidden0, d_hidden0, d_low0, hidden1, d_hidden1, d_low1, halves, pull_out, bias_sum, go_sum, out_sum, encoded, layer, sems):
    unpack(rec_ref, fields)
    pulls[...] = jnp.transpose(ret_ref[...])
    total = count_pairs(fields, halves)

    def copies(n):
        slot = lax.rem(n, RING_IN)
        return (
            pltpu.make_async_copy(encoded_ref.at[n], encoded.at[slot], sems.at[0, slot]),
            pltpu.make_async_copy(layer_ref.at[n], layer.at[slot], sems.at[1, slot]),
        )

    def fetch(n, _):
        for copy in copies(n):
            copy.start()
        return 0

    lax.fori_loop(0, jnp.minimum(RING_IN - 2, total), fetch, 0)
    for zeroed in (gh_ref, go_sum, bias_sum, out_sum, hidden1, d_hidden1, d_low1):
        zeroed[...] = jnp.zeros_like(zeroed)
    pull_out[SLOTS:] = jnp.zeros((4, 8 * S, LANES), F32)

    def prepare(p, _):
        four = pulls[pl.ds(pl.multiple_of(p * 8, 8), 8), :]
        g = jnp.concatenate([four[0:4], four[4:8]], axis=1)
        coef = coef_ref[p]
        part = [coef[n * S : (n + 1) * S] for n in range(7)]
        outs = [part[0] * g[0:1] + part[1] * g[1:2] + part[2] * g[2:3] + part[3] * g[3:4]]
        outs += [part[4 + c] * g[c : c + 1] for c in range(3)]
        zeros = jnp.zeros((S, LANES), F32)
        for f in range(4):
            out_sum[f * S : (f + 1) * S, :] += outs[f]
            for h in range(2):
                pull_out[2 * p + h, pl.ds(f, S, stride=8), :] = outs[f][:, h * LANES : (h + 1) * LANES]
                pull_out[2 * p + h, pl.ds(f + 4, S, stride=8), :] = zeros
        return 0

    lax.fori_loop(0, TILES, prepare, 0)

    products = ((hidden0, d_hidden0, d_low0), (hidden1, d_hidden1, d_low1))

    def run(t, now, before, older, parity):
        @pl.when(t < total)
        def _():
            for copy in copies(t):
                copy.wait()

        @pl.when(t + RING_IN - 2 < total)
        def _():
            for copy in copies(t + RING_IN - 2):
                copy.start()

        place = lax.rem(jnp.minimum(t, total - 1), RING_IN)
        earlier = lax.rem(jnp.maximum(jnp.minimum(t - 1, total - 1), 0), RING_IN)
        hidden1, d_hidden1, d_low1 = products[1 - parity]
        hidden, d_hidden, d_low = products[parity]
        wot = wot_ref[:, 0:16]
        q, i = now
        rows = pl.ds(pl.multiple_of(i * 16, 16), 16)
        four = [pull_out[4 * q + h, rows, :] for h in range(4)]
        chunks = [slice(n * 256, (n + 1) * 256) for n in range(4)]

        def pulled(n):
            d = jnp.concatenate(four[n % 2 * 2 : n % 2 * 2 + 2], axis=1)
            d = d[n // 2 * 8 : n // 2 * 8 + 8]
            low = jnp.concatenate([d, jnp.zeros_like(d)], axis=0).astype(BF16)
            d_low[:, chunks[n]] = low
            return nn(wot, low)

        def activate(n, d):
            v = layer[place, :, chunks[n]].astype(F32)
            t = jnp.tanh(v)
            u = t + 1.0
            h = v * u
            slope = u + h * (1.0 - t)
            d_pre = d * slope
            d_hidden[:, chunks[n]] = d_pre.astype(BF16)
            hidden[:, chunks[n]] = h.astype(BF16)
            return d_pre[:, 0:LANES] + d_pre[:, LANES:]

        summed = bias_sum[...]
        d = pulled(0)
        for n in range(4):
            following = pulled(n + 1) if n < 3 else None
            gh_ref[...] += nt(encoded[earlier, :, chunks[n]], d_hidden1[:, chunks[n]])
            summed = summed + activate(n, d)
            go_sum[...] += nt(d_low1[:, chunks[n]], hidden1[:, chunks[n]])[0:8]
            d = following
        bias_sum[...] = summed

    turns = jnp.where(total > 0, (total + 2) // 2, 0)
    walk(None, halves, total, turns, run)
    go_ref[...] = go_sum[0:4]
    folded = jnp.transpose(bias_sum[...])
    gb_ref[...] = jnp.sum(folded, axis=0, keepdims=True)
    sums = [
        jnp.sum(out_sum[f * S : (f + 1) * S, :], axis=(0, 1), keepdims=True)
        for f in range(4)
    ]
    lane = iota((1, 4), 1)
    row = jnp.zeros((1, 4), F32)
    for f in range(4):
        row = jnp.where(lane == f, sums[f], row)
    gob_ref[...] = row


def sds(*shape, dtype=F32):
    return jax.ShapeDtypeStruct(shape, dtype)


def call(kernel, out_shape, scratch=(), in_specs=None, flops=0, transcendentals=0, touched=1 << 20, vmem=6.0, out_specs=None):
    extra = {} if in_specs is None else {"in_specs": in_specs}
    if out_specs is not None:
        extra["out_specs"] = out_specs
    return pl.pallas_call(
        kernel,
        out_shape=out_shape,
        **extra,
        scratch_shapes=list(scratch),
        compiler_params=pltpu.CompilerParams(vmem_limit_bytes=int(vmem * (1 << 20))),
        cost_estimate=pl.CostEstimate(
            flops=flops, bytes_accessed=touched, transcendentals=transcendentals
        ),
    )


VM = pl.BlockSpec(memory_space=pltpu.VMEM)
HBM = pl.BlockSpec(memory_space=pl.ANY)
FAR = pl.BlockSpec(memory_space=pltpu.HBM)


def phase_scratch():
    return [
        pltpu.VMEM((256, 512), F32),
        pltpu.VMEM((256, 512), F32),
        pltpu.VMEM((LANES, 512), F32),
    ]


def region_forward(received, turns, w_t, bias_cols, wo, b_out):
    wide = pltpu.VMEM((256, 1024), BF16)
    return call(
        forward_kernel,
        (
            sds(received.shape[0] // 2, LANES),
            sds(SLOTS + 4, 8 * S, LANES),
            sds(STEPS + 2, 256, 1024, dtype=BF16),
            sds(STEPS + 2, 256, 1024, dtype=BF16),
        ),
        [pltpu.VMEM((PAD * 8, LANES), F32)]
        + phase_scratch()
        + [wide] * 2
        + [pltpu.VMEM((RING_OUT // 2, 256, 1024), BF16)] * 2
        + [pltpu.VMEM((RING_OUT, 256, 1024), BF16)]
        + [
            pltpu.SMEM((GROUPS,), jnp.int32),
            pltpu.VMEM((LANES, LANES), F32),
            pltpu.SemaphoreType.DMA((2, RING_OUT)),
        ],
        out_specs=(VM, VM, FAR, FAR),
        in_specs=[VM] * 6,
        flops=7 * 10**9,
        vmem=44.0,
    )(received, turns, w_t, bias_cols, wo, b_out)


def region_middle(received, raw, b_out):
    return call(
        middle_kernel,
        sds(TILES, 7 * S, 256),
        [pltpu.VMEM((PAD * 8, LANES), F32)],
        in_specs=[VM] * 3,
        vmem=4.0,
    )(received, raw, b_out)


def region_backward(received, returned, wo_t, coef, encoded, layer):
    wide = pltpu.VMEM((256, 1024), BF16)
    return call(
        backward_kernel,
        (sds(256, 256), sds(1, 256), sds(4, 256), sds(1, 4)),
        [pltpu.VMEM((PAD * 8, LANES), F32), pltpu.VMEM((LANES, LANES), F32)]
        + [wide, wide, pltpu.VMEM((16, 1024), BF16)] * 2
        + [
            pltpu.SMEM((GROUPS,), jnp.int32),
            pltpu.VMEM((SLOTS + 4, 8 * S, LANES), F32),
            pltpu.VMEM((256, LANES), F32),
            pltpu.VMEM((8, 256), F32),
            pltpu.VMEM((4 * S, 256), F32),
            pltpu.VMEM((RING_IN, 256, 1024), BF16),
            pltpu.VMEM((RING_IN, 256, 1024), BF16),
            pltpu.SemaphoreType.DMA((2, RING_IN)),
        ],
        in_specs=[VM] * 4 + [HBM] * 2,
        flops=20 * 10**9,
        vmem=44.0,
    )(received, returned, wo_t, coef, encoded, layer)


def exchange(x):
    return lax.all_to_all(x, BOTH, split_axis=0, concat_axis=0, tiled=True)


def shards(anchors, directions, regions, counts, seg_len, color_grad, frequencies, w_hidden, b_hidden, w_out, b_out):
    count = lax.axis_size("rx") * lax.axis_size("ry")
    rays = regions.shape[0]
    region_rows = regions.T
    outbound, slot = call(
        pack_kernel,
        (sds(count * 2, LANES), sds(1, rays * K)),
        [
            pltpu.VMEM((rays * K, LANES), F32),
            pltpu.VMEM((K, rays), jnp.int32),
            pltpu.VMEM((K, rays), jnp.int32),
            pltpu.VMEM((3, rays), F32),
            pltpu.VMEM((3, rays), F32),
            pltpu.VMEM((K, rays), F32),
            pltpu.SemaphoreType.DMA((5,)),
        ],
        in_specs=[FAR] * 5,
        vmem=60.0,
    )(region_rows, counts.T, anchors, directions, seg_len)
    turns, w_t, bias_cols, wo_t, wo, out_rows = call(
        setup_kernel,
        (
            sds(3, LANES, LANES),
            sds(256, 256, dtype=BF16),
            sds(256, LANES),
            sds(256, LANES, dtype=BF16),
            sds(16, 256, dtype=BF16),
            sds(8, 256),
        ),
    )(frequencies[0], w_hidden[0], b_hidden, w_out[0], b_out)
    received = exchange(outbound)
    reply, raw, encoded, layer = region_forward(received, turns, w_t, bias_cols, wo, out_rows)
    arrived = exchange(reply)
    coef = region_middle(received, raw, out_rows)
    colour, returning = call(
        combine_kernel,
        (sds(3, rays), sds(count, LANES)),
        vmem=5.0,
    )(region_rows, slot, color_grad, arrived)
    returned = exchange(returning)
    gh, gb, go, gob = region_backward(received, returned, wo_t, coef, encoded, layer)
    return (colour, gh[None], gb, go[None], gob)


def solution(mesh):
    spread = P(BOTH)
    in_specs = (
        P(None, BOTH),
        P(None, BOTH),
        spread,
        spread,
        P(None, BOTH),
        P(None, BOTH),
        spread,
        spread,
        spread,
        spread,
        spread,
    )
    out_specs = (P(None, BOTH), spread, spread, spread, spread)
    return jax.shard_map(
        shards, mesh=mesh, in_specs=in_specs, out_specs=out_specs, check_vma=False
    )
```

```python
import functools

import jax
import jax.numpy as jnp
from jax import lax
from jax.experimental import pallas as pl
from jax.experimental.pallas import tpu as pltpu
from jax.sharding import PartitionSpec as P

S = 16
K = 4
SLOTS = 24
PAD = 32
TILES = SLOTS // 2
GROUPS = SLOTS // 4
STEPS = GROUPS * S // 2
RING_OUT = 8
RING_IN = 16
LANES = 128
BOTH = ("rx", "ry")
F32 = jnp.float32
BF16 = jnp.bfloat16
SIN = (3.14159264, -5.16771009, 2.55007766, -0.59829216, 0.07765941)
COS = (0.99999995, -4.93479286, 4.05841191, -1.33188016, 0.21969679)
TURN = 0.15915494309189535


def iota(shape, axis):
    return lax.broadcasted_iota(jnp.int32, shape, axis)


def nt(a, b):
    return lax.dot_general(a, b, (((1,), (1,)), ((), ())), preferred_element_type=F32)


def nn(a, b):
    return lax.dot_general(a, b, (((1,), (0,)), ((), ())), preferred_element_type=F32)


def split3(x):
    hi = x.astype(BF16).astype(F32)
    rest = x - hi
    mid = rest.astype(BF16).astype(F32)
    return (hi, mid, rest - mid)


def split2(x):
    return split3(x)[0:2]


LEAD_SIN = (3.14159028, -5.1674077, 2.54402081, -0.5594899)
LEAD_COS = (0.9999933, -4.93393801, 4.04128381, -1.22212701)


def lead_turns(u):
    f = u - jnp.round(u)
    q = f * f
    s = f * (LEAD_SIN[0] + q * (LEAD_SIN[1] + q * (LEAD_SIN[2] + q * LEAD_SIN[3])))
    c = LEAD_COS[0] + q * (LEAD_COS[1] + q * (LEAD_COS[2] + q * LEAD_COS[3]))
    s2 = s + s
    return s2 * c, 1.0 - s2 * s


def sincos_turns(u):
    f = u - jnp.round(u)
    q = f * f
    s = f * (SIN[0] + q * (SIN[1] + q * (SIN[2] + q * (SIN[3] + q * SIN[4]))))
    c = COS[0] + q * (COS[1] + q * (COS[2] + q * (COS[3] + q * COS[4])))
    s2 = s + s
    return s2 * c, 1.0 - s2 * s


def per_segment(rows):
    return jnp.concatenate([rows[k : k + 1] for k in range(K)], axis=1)


def one_hot_regions(region, count):
    return jnp.where(iota((count, region.shape[1]), 0).astype(F32) == region, 1.0, 0.0)


def scatter(onehot, slot, fields, split):
    n = fields.shape[0]
    total = None
    owner = (iota((SLOTS * n, slot.shape[1]), 0) // n).astype(F32) == slot
    rest = jnp.zeros(((PAD - SLOTS) * n, slot.shape[1]), BF16)
    for part in split(fields):
        spread = jnp.where(owner, jnp.concatenate([part] * SLOTS, axis=0), 0.0).astype(BF16)
        piece = nt(onehot, jnp.concatenate([spread, rest], axis=0))
        total = piece if total is None else total + piece
    return total


def pack_kernel(region_in, count_in, anchor_in, direction_in, length_in, out_ref, slot_ref, column, region_ref, count_ref, anchor_ref, direction_ref, length_ref, sems):
    sources = (region_in, count_in, anchor_in, direction_in, length_in)
    places = (region_ref, count_ref, anchor_ref, direction_ref, length_ref)
    copies = [
        pltpu.make_async_copy(source, place, sems.at[n])
        for n, (source, place) in enumerate(zip(sources, places))
    ]
    for copy in copies:
        copy.start()
    for copy in copies:
        copy.wait()
    region = per_segment(region_ref[...].astype(F32))
    live = count_ref[...].astype(F32)
    lengths = length_ref[...]
    blocks = []
    start = jnp.full((1, lengths.shape[1]), 0.5, F32)
    for k in range(K):
        length = lengths[k : k + 1]
        spacing = length / jnp.maximum(live[k : k + 1], 1.0)
        first = start + 0.5 * spacing
        points = anchor_ref[...] + first * direction_ref[...]
        steps = spacing * direction_ref[...]
        blocks.append(jnp.concatenate([points, steps, spacing, live[k : k + 1]], axis=0))
        start = start + length
    fields = jnp.concatenate(blocks, axis=1)
    segments = fields.shape[1]
    regions = out_ref.shape[0] // 2
    key = (
        region * 32768.0
        + (fields[7:8] - 1.0) * 2048.0
        + iota((1, segments), 1).astype(F32)
    )
    for c in range(segments // LANES):
        chunk = key[:, c * LANES : (c + 1) * LANES]
        column[c * LANES : (c + 1) * LANES, :] = jnp.transpose(
            jnp.broadcast_to(chunk, (LANES, LANES))
        )
    onehot = one_hot_regions(region, regions)
    sizes = jnp.sum(onehot, axis=1, keepdims=True)
    above = jnp.sum(
        jnp.where(iota((regions, segments), 0).astype(F32) > region, sizes, 0.0),
        axis=0,
        keepdims=True,
    )
    larger = []
    for c in range(segments // LANES):
        chunk = key[:, c * LANES : (c + 1) * LANES]
        larger.append(
            jnp.sum(jnp.where(column[...] > chunk, 1.0, 0.0), axis=0, keepdims=True)
        )
    slot = jnp.concatenate(larger, axis=1) - above
    slot_ref[...] = slot
    packed = scatter(onehot.astype(BF16), slot, fields, split3)
    for h in range(2):
        out_ref[pl.ds(h, regions, stride=2), :] = packed[:, h * LANES : (h + 1) * LANES]


def unpack(rec_ref, fields):
    for h in range(2):
        rows = rec_ref[pl.ds(h, rec_ref.shape[0] // 2, stride=2), :]
        fields[h * LANES : (h + 1) * LANES, :] = jnp.transpose(rows)


def combine_kernel(region_ref, slot_ref, grad_ref, arrived_ref, colour_ref, out_ref):
    region = per_segment(region_ref[...].astype(F32))
    slot = slot_ref[...]
    regions = arrived_ref.shape[0]
    onehot = one_hot_regions(region, regions).astype(BF16)
    taken = None
    for part in split2(jnp.transpose(arrived_ref[...])[0 : SLOTS * 4]):
        piece = nn(part.astype(BF16), onehot)
        taken = piece if taken is None else taken + piece
    rows = taken.shape[0]
    kept = jnp.where((iota(taken.shape, 0) // 4).astype(F32) == slot, taken, 0.0)
    total = kept[0:8]
    for r in range(8, rows, 8):
        total = total + kept[r : r + 8]
    values = total[0:4] + total[4:8]
    rays = grad_ref.shape[1]
    grad = grad_ref[...]
    seen = [jnp.ones((1, rays), F32)]
    colours = []
    for k in range(K):
        block = values[:, k * rays : (k + 1) * rays]
        colours.append(block[1:4])
        seen.append(seen[-1] * block[0:1])
    colour = seen[0] * colours[0]
    for k in range(1, K):
        colour = colour + seen[k] * colours[k]
    colour_ref[...] = colour
    behind = jnp.zeros((1, rays), F32)
    replies = [None] * K
    for k in reversed(range(K)):
        replies[k] = jnp.concatenate([grad * seen[k], behind], axis=0)
        pulled = grad * colours[k]
        behind = behind + seen[k] * (pulled[0:1] + pulled[1:2] + pulled[2:3])
    out_ref[...] = scatter(onehot, slot, jnp.concatenate(replies, axis=1), split2)


def setup_kernel(freq_ref, w_ref, bias_ref, w_out_ref, out_bias_ref, turns_ref, wt_ref, bias_cols_ref, wot_ref, wo_ref, out_rows_ref):
    b = out_bias_ref[...]
    rows = [jnp.broadcast_to(b[:, f : f + 1], (1, 256)) for f in range(4)]
    out_rows_ref[...] = jnp.concatenate(rows + rows, axis=0)
    for c in range(3):
        turns_ref[c] = jnp.transpose(
            jnp.broadcast_to(freq_ref[c : c + 1, :] * TURN, (LANES, LANES))
        )
    wt_ref[...] = (0.5 * jnp.transpose(w_ref[...].astype(F32))).astype(BF16)
    for h in range(2):
        bias_cols_ref[h * LANES : (h + 1) * LANES, :] = jnp.transpose(
            0.5 * jnp.broadcast_to(bias_ref[:, h * LANES : (h + 1) * LANES], (LANES, LANES))
        )
    padded = jnp.concatenate([w_out_ref[...].astype(F32), jnp.zeros((12, 256), F32)], axis=0)
    wo_ref[...] = padded.astype(BF16)
    wide = jnp.concatenate([padded, jnp.zeros((LANES - 16, 256), F32)], axis=0)
    wot_ref[...] = (0.5 * jnp.transpose(wide)).astype(BF16)


def tile_fields(fields, p):
    two = fields[pl.ds(pl.multiple_of(p * 16, 16), 16), :]
    return jnp.concatenate([two[0:8], two[8:16]], axis=1)


def start_phases(fields, q, turns_ref, even, odd, twice):
    for h in range(4):
        x = fields[pl.ds(pl.multiple_of(q * 32 + h * 8, 8), 8), :]
        lanes = slice(h * LANES, (h + 1) * LANES)
        for r in range(4):
            rows = slice(r * 32, (r + 1) * 32)
            turns = [turns_ref[c, rows, :] for c in range(3)]
            s0, c0 = lead_turns(turns[0] * x[0:1] + turns[1] * x[1:2] + turns[2] * x[2:3])
            sd, cd = sincos_turns(turns[0] * x[3:4] + turns[1] * x[4:5] + turns[2] * x[5:6])
            low = slice(LANES + r * 32, LANES + (r + 1) * 32)
            even[rows, lanes] = s0
            even[low, lanes] = c0
            odd[rows, lanes] = s0 * cd - c0 * sd
            odd[low, lanes] = c0 * cd + s0 * sd
            twice[rows, lanes] = cd + cd


def encode_pair(even, odd, twice, encoded, quarters=range(4)):
    for r in quarters:
        rows = slice(r * 32, (r + 1) * 32)
        for h in range(4):
            lanes = slice(h * LANES, (h + 1) * LANES)
            k = twice[rows, lanes]
            for part in (rows, slice(LANES + r * 32, LANES + (r + 1) * 32)):
                now, last = even[part, lanes], odd[part, lanes]
                following = k * now - last
                even[part, lanes] = k * following - now
                odd[part, lanes] = following
                encoded[part, lanes] = now.astype(BF16)
                encoded[part, 512 + h * LANES : 512 + (h + 1) * LANES] = following.astype(BF16)


def count_pairs(fields, halves):
    total = jnp.int32(0)
    for q in range(GROUPS):
        most = [fields[q * 32 + h * 8 + 7 : q * 32 + h * 8 + 8, :] for h in range(4)]
        most = jnp.maximum(jnp.maximum(most[0], most[1]), jnp.maximum(most[2], most[3]))
        half = (jnp.max(most).astype(jnp.int32) + 1) // 2
        halves[q] = half
        total = total + half
    return total


def walk(start, halves, total, turns, run):
    nowhere = (jnp.int32(GROUPS), jnp.int32(0))

    def body(turn, carry):
        q, i, before, older = carry
        for parity in range(2):
            valid = 2 * turn + parity < total
            now = (jnp.where(valid, q, GROUPS), jnp.where(valid, i, 0))

            if start is not None:
                fresh = jnp.logical_and(valid, i == 0).astype(jnp.int32)
                lax.fori_loop(0, fresh, functools.partial(start, q), 0)
            more = i + 1 < halves[jnp.minimum(q, GROUPS - 1)]
            q = jnp.where(more, q, q + 1)
            i = jnp.where(more, i + 1, 0)
            run(2 * turn + parity, now, before, older, parity)
            before, older = now, before
        return (q, i, before, older)

    carry = (jnp.int32(0), jnp.int32(0), nowhere, nowhere)
    lax.fori_loop(0, turns, body, carry)


def sigmoid(v):
    return 0.5 * jnp.tanh(0.5 * v) + 0.5


def softplus(v):
    return jnp.maximum(v, 0.0) + jnp.log1p(jnp.exp(-jnp.abs(v)))


def running_sum(x):
    row = iota(x.shape, 0)
    for shift in (1, 2, 4, 8):
        x = x + jnp.where(row >= shift, pltpu.roll(x, shift, 0), 0.0)
    return x


def absorbed(q):
    small = q * (1.0 - q * (0.5 - q * (1.0 / 6.0 - q * (1.0 / 24.0))))
    return jnp.where(q < 0.03, small, 1.0 - jnp.exp(-q))


def shade(raw, p, x, bias_ref):
    live = iota((S, 256), 0).astype(F32) < x[7:8]
    spacing = jnp.where(live, x[6:7], 0.0)
    outs = []
    for f in range(4):
        pair = [raw[2 * p + h, pl.ds(f, S, stride=8), :] for h in range(2)]
        outs.append(jnp.where(live, jnp.concatenate(pair, axis=1), 0.0) + bias_ref[f : f + 1, :])
    sigma = softplus(outs[0])
    colours = [sigmoid(v) for v in outs[1:]]
    q = sigma * spacing
    through = running_sum(q)
    weight = jnp.exp(q - through) * absorbed(q)
    return outs[0], colours, spacing, through, weight


def forward_kernel(rec_ref, turns_ref, wt_ref, bias_ref, wo_ref, out_bias_ref, reply_ref, raw_ref, encoded_ref, layer_ref, fields, even, odd, twice, hidden0, hidden1, encoded0, encoded1, layer, halves, reply, sems):
    unpack(rec_ref, fields)
    reply[...] = jnp.zeros_like(reply)
    for zeroed in (hidden0, hidden1):
        zeroed[...] = jnp.zeros_like(zeroed)

    total = count_pairs(fields, halves)
    hidden = (hidden0, hidden1)

    encoded = (encoded0, encoded1)

    def copy(which, n, parity):
        slot = lax.rem(n, RING_OUT)
        held = layer.at[slot] if which else encoded[parity].at[lax.div(slot, 2)]
        kept = layer_ref if which else encoded_ref
        return pltpu.make_async_copy(held, kept.at[n], sems.at[which, slot])

    def keep(due, which, n, begin, parity):
        @pl.when(due)
        def _():
            if begin:
                copy(which, n, parity).start()
            else:
                copy(which, n, parity).wait()

    def start(q, _, unused):
        start_phases(fields, q, turns_ref, even, odd, twice)
        return 0

    def run(t, now, before, older, parity):
        other = 1 - parity
        fresh = encoded[parity].at[lax.div(lax.rem(t, RING_OUT), 2)]
        place = lax.rem(t + RING_OUT - 1, RING_OUT)
        behind = lax.div(place, 2)
        keep(t >= RING_OUT, 0, t - RING_OUT, False, parity)
        keep(t > RING_OUT, 1, t - 1 - RING_OUT, False, other)
        keep(t >= 1, 0, t - 1, True, other)
        keep(t >= 2, 1, t - 2, True, parity)
        bias = jnp.concatenate([bias_ref[...]] * 2, axis=1)
        wt = wt_ref[...]
        chunks = [slice(n * 256, (n + 1) * 256) for n in range(4)]

        def activate(n, v):
            hidden[other][:, chunks[n]] = (v * jnp.tanh(v) + v).astype(BF16)
            layer[place, :, chunks[n]] = v.astype(BF16)

        def worked(n):
            return nn(wt, encoded[other][behind, :, chunks[n]]) + bias

        q, i = older
        rows = pl.ds(pl.multiple_of(i * 16, 16), 16)
        outs = []
        v = worked(0)
        encode_pair(even, odd, twice, fresh, [0])
        for n in range(4):
            following = worked(n + 1) if n < 3 else None
            activate(n, v)
            if n < 3:
                encode_pair(even, odd, twice, fresh, [n + 1])
            v = following
        wide = nn(wo_ref[...], hidden[parity][...])[0:8]
        outs = [wide[:, c] for c in chunks]
        for h in range(4):
            lanes = slice(h % 2 * LANES, (h % 2 + 1) * LANES)
            raw_ref[4 * q + h, rows, :] = jnp.concatenate(
                [outs[h // 2][:, lanes], outs[2 + h // 2][:, lanes]], axis=0
            )

    turns = (total + 3) // 2
    walk(start, halves, total, turns, run)
    steps = 2 * turns

    def drain(which, n, _):
        for parity in range(2):
            keep(lax.rem(n, 2) == parity, which, n, False, parity)
        return 0

    lax.fori_loop(jnp.maximum(steps - RING_OUT, 0), steps - 1, functools.partial(drain, 0), 0)
    lax.fori_loop(jnp.maximum(steps - 1 - RING_OUT, 0), steps - 2, functools.partial(drain, 1), 0)

    def finish(p, _):
        x = tile_fields(fields, p)
        _, colours, _, through, weight = shade(raw_ref, p, x, out_bias_ref)
        local = [jnp.exp(-through[S - 1 : S])] + [
            jnp.sum(weight * c, axis=0, keepdims=True) for c in colours
        ]
        block = jnp.concatenate(local, axis=0)
        reply[pl.ds(pl.multiple_of(p * 8, 8), 8), :] = jnp.concatenate(
            [block[:, 0:LANES], block[:, LANES:]], axis=0
        )
        return 0

    lax.fori_loop(0, TILES, finish, 0)
    reply_ref[...] = jnp.transpose(reply[...])


def middle_kernel(rec_ref, raw_ref, out_bias_ref, coef_ref, fields):
    unpack(rec_ref, fields)

    def tile(p, _):
        x = tile_fields(fields, p)
        out0, colours, spacing, through, weight = shade(raw_ref, p, x, out_bias_ref)
        scale = spacing * sigmoid(out0)
        left = jnp.exp(-through)
        parts = []
        for c in colours:
            seen = running_sum(weight * c)
            later = seen[S - 1 : S] - seen
            parts.append(scale * (c * left - later))
        parts.append(-scale)
        for c in colours:
            parts.append(weight * c * (1.0 - c))
        coef_ref[p] = jnp.concatenate(parts, axis=0)
        return 0

    lax.fori_loop(0, SLOTS // 2, tile, 0)


def backward_kernel(rec_ref, ret_ref, wot_ref, coef_ref, encoded_ref, layer_ref, gh_ref, gb_ref, go_ref, gob_ref, fields, pulls, hidden0, d_hidden0, d_low0, hidden1, d_hidden1, d_low1, halves, pull_out, bias_sum, go_sum, out_sum, encoded, layer, sems):
    unpack(rec_ref, fields)
    pulls[...] = jnp.transpose(ret_ref[...])
    total = count_pairs(fields, halves)

    def copies(n):
        slot = lax.rem(n, RING_IN)
        return (
            pltpu.make_async_copy(encoded_ref.at[n], encoded.at[slot], sems.at[0, slot]),
            pltpu.make_async_copy(layer_ref.at[n], layer.at[slot], sems.at[1, slot]),
        )

    def fetch(n, _):
        for copy in copies(n):
            copy.start()
        return 0

    lax.fori_loop(0, jnp.minimum(RING_IN - 2, total), fetch, 0)
    for zeroed in (gh_ref, go_sum, bias_sum, out_sum, hidden1, d_hidden1, d_low1):
        zeroed[...] = jnp.zeros_like(zeroed)
    pull_out[SLOTS:] = jnp.zeros((4, 8 * S, LANES), F32)

    def prepare(p, _):
        four = pulls[pl.ds(pl.multiple_of(p * 8, 8), 8), :]
        g = jnp.concatenate([four[0:4], four[4:8]], axis=1)
        coef = coef_ref[p]
        part = [coef[n * S : (n + 1) * S] for n in range(7)]
        outs = [part[0] * g[0:1] + part[1] * g[1:2] + part[2] * g[2:3] + part[3] * g[3:4]]
        outs += [part[4 + c] * g[c : c + 1] for c in range(3)]
        zeros = jnp.zeros((S, LANES), F32)
        for f in range(4):
            out_sum[f * S : (f + 1) * S, :] += outs[f]
            for h in range(2):
                pull_out[2 * p + h, pl.ds(f, S, stride=8), :] = outs[f][:, h * LANES : (h + 1) * LANES]
                pull_out[2 * p + h, pl.ds(f + 4, S, stride=8), :] = zeros
        return 0

    lax.fori_loop(0, TILES, prepare, 0)

    products = ((hidden0, d_hidden0, d_low0), (hidden1, d_hidden1, d_low1))

    def run(t, now, before, older, parity):
        @pl.when(t < total)
        def _():
            for copy in copies(t):
                copy.wait()

        @pl.when(t + RING_IN - 2 < total)
        def _():
            for copy in copies(t + RING_IN - 2):
                copy.start()

        place = lax.rem(jnp.minimum(t, total - 1), RING_IN)
        earlier = lax.rem(jnp.maximum(jnp.minimum(t - 1, total - 1), 0), RING_IN)
        hidden1, d_hidden1, d_low1 = products[1 - parity]
        hidden, d_hidden, d_low = products[parity]
        wot = wot_ref[:, 0:16]
        q, i = now
        rows = pl.ds(pl.multiple_of(i * 16, 16), 16)
        four = [pull_out[4 * q + h, rows, :] for h in range(4)]
        chunks = [slice(n * 256, (n + 1) * 256) for n in range(4)]

        def pulled(n):
            d = jnp.concatenate(four[n % 2 * 2 : n % 2 * 2 + 2], axis=1)
            d = d[n // 2 * 8 : n // 2 * 8 + 8]
            low = jnp.concatenate([d, jnp.zeros_like(d)], axis=0).astype(BF16)
            d_low[:, chunks[n]] = low
            return nn(wot, low)

        def activate(n, d):
            v = layer[place, :, chunks[n]].astype(F32)
            t = jnp.tanh(v)
            u = t + 1.0
            h = v * u
            slope = u + h * (1.0 - t)
            d_pre = d * slope
            d_hidden[:, chunks[n]] = d_pre.astype(BF16)
            hidden[:, chunks[n]] = h.astype(BF16)
            return d_pre[:, 0:LANES] + d_pre[:, LANES:]

        summed = bias_sum[...]
        d = pulled(0)
        for n in range(4):
            following = pulled(n + 1) if n < 3 else None
            if n % 2 == 0:
                both = slice(n * 256, (n + 2) * 256)
                gh_ref[...] += nt(encoded[earlier, :, both], d_hidden1[:, both])
            summed = summed + activate(n, d)
            go_sum[...] += nt(d_low1[:, chunks[n]], hidden1[:, chunks[n]])[0:8]
            d = following
        bias_sum[...] = summed

    turns = jnp.where(total > 0, (total + 2) // 2, 0)
    walk(None, halves, total, turns, run)
    go_ref[...] = go_sum[0:4]
    folded = jnp.transpose(bias_sum[...])
    gb_ref[...] = jnp.sum(folded, axis=0, keepdims=True)
    sums = [
        jnp.sum(out_sum[f * S : (f + 1) * S, :], axis=(0, 1), keepdims=True)
        for f in range(4)
    ]
    lane = iota((1, 4), 1)
    row = jnp.zeros((1, 4), F32)
    for f in range(4):
        row = jnp.where(lane == f, sums[f], row)
    gob_ref[...] = row


def sds(*shape, dtype=F32):
    return jax.ShapeDtypeStruct(shape, dtype)


def call(kernel, out_shape, scratch=(), in_specs=None, flops=0, transcendentals=0, touched=1 << 20, vmem=6.0, out_specs=None):
    extra = {} if in_specs is None else {"in_specs": in_specs}
    if out_specs is not None:
        extra["out_specs"] = out_specs
    return pl.pallas_call(
        kernel,
        out_shape=out_shape,
        **extra,
        scratch_shapes=list(scratch),
        compiler_params=pltpu.CompilerParams(vmem_limit_bytes=int(vmem * (1 << 20))),
        cost_estimate=pl.CostEstimate(
            flops=flops, bytes_accessed=touched, transcendentals=transcendentals
        ),
    )


VM = pl.BlockSpec(memory_space=pltpu.VMEM)
HBM = pl.BlockSpec(memory_space=pl.ANY)
FAR = pl.BlockSpec(memory_space=pltpu.HBM)


def phase_scratch():
    return [
        pltpu.VMEM((256, 512), F32),
        pltpu.VMEM((256, 512), F32),
        pltpu.VMEM((LANES, 512), F32),
    ]


def region_forward(received, turns, w_t, bias_cols, wo, b_out):
    wide = pltpu.VMEM((256, 1024), BF16)
    return call(
        forward_kernel,
        (
            sds(received.shape[0] // 2, LANES),
            sds(SLOTS + 4, 8 * S, LANES),
            sds(STEPS + 2, 256, 1024, dtype=BF16),
            sds(STEPS + 2, 256, 1024, dtype=BF16),
        ),
        [pltpu.VMEM((PAD * 8, LANES), F32)]
        + phase_scratch()
        + [wide] * 2
        + [pltpu.VMEM((RING_OUT // 2, 256, 1024), BF16)] * 2
        + [pltpu.VMEM((RING_OUT, 256, 1024), BF16)]
        + [
            pltpu.SMEM((GROUPS,), jnp.int32),
            pltpu.VMEM((LANES, LANES), F32),
            pltpu.SemaphoreType.DMA((2, RING_OUT)),
        ],
        out_specs=(VM, VM, FAR, FAR),
        in_specs=[VM] * 6,
        flops=7 * 10**9,
        vmem=44.0,
    )(received, turns, w_t, bias_cols, wo, b_out)


def region_middle(received, raw, b_out):
    return call(
        middle_kernel,
        sds(TILES, 7 * S, 256),
        [pltpu.VMEM((PAD * 8, LANES), F32)],
        in_specs=[VM] * 3,
        vmem=4.0,
    )(received, raw, b_out)


def region_backward(received, returned, wo_t, coef, encoded, layer):
    wide = pltpu.VMEM((256, 1024), BF16)
    return call(
        backward_kernel,
        (sds(256, 256), sds(1, 256), sds(4, 256), sds(1, 4)),
        [pltpu.VMEM((PAD * 8, LANES), F32), pltpu.VMEM((LANES, LANES), F32)]
        + [wide, wide, pltpu.VMEM((16, 1024), BF16)] * 2
        + [
            pltpu.SMEM((GROUPS,), jnp.int32),
            pltpu.VMEM((SLOTS + 4, 8 * S, LANES), F32),
            pltpu.VMEM((256, LANES), F32),
            pltpu.VMEM((8, 256), F32),
            pltpu.VMEM((4 * S, 256), F32),
            pltpu.VMEM((RING_IN, 256, 1024), BF16),
            pltpu.VMEM((RING_IN, 256, 1024), BF16),
            pltpu.SemaphoreType.DMA((2, RING_IN)),
        ],
        in_specs=[VM] * 4 + [HBM] * 2,
        flops=20 * 10**9,
        vmem=44.0,
    )(received, returned, wo_t, coef, encoded, layer)


def exchange(x):
    return lax.all_to_all(x, BOTH, split_axis=0, concat_axis=0, tiled=True)


def shards(anchors, directions, regions, counts, seg_len, color_grad, frequencies, w_hidden, b_hidden, w_out, b_out):
    count = lax.axis_size("rx") * lax.axis_size("ry")
    rays = regions.shape[0]
    region_rows = regions.T
    outbound, slot = call(
        pack_kernel,
        (sds(count * 2, LANES), sds(1, rays * K)),
        [
            pltpu.VMEM((rays * K, LANES), F32),
            pltpu.VMEM((K, rays), jnp.int32),
            pltpu.VMEM((K, rays), jnp.int32),
            pltpu.VMEM((3, rays), F32),
            pltpu.VMEM((3, rays), F32),
            pltpu.VMEM((K, rays), F32),
            pltpu.SemaphoreType.DMA((5,)),
        ],
        in_specs=[FAR] * 5,
        vmem=60.0,
    )(region_rows, counts.T, anchors, directions, seg_len)
    turns, w_t, bias_cols, wo_t, wo, out_rows = call(
        setup_kernel,
        (
            sds(3, LANES, LANES),
            sds(256, 256, dtype=BF16),
            sds(256, LANES),
            sds(256, LANES, dtype=BF16),
            sds(16, 256, dtype=BF16),
            sds(8, 256),
        ),
    )(frequencies[0], w_hidden[0], b_hidden, w_out[0], b_out)
    received = exchange(outbound)
    reply, raw, encoded, layer = region_forward(received, turns, w_t, bias_cols, wo, out_rows)
    arrived = exchange(reply)
    coef = region_middle(received, raw, out_rows)
    colour, returning = call(
        combine_kernel,
        (sds(3, rays), sds(count, LANES)),
        vmem=5.0,
    )(region_rows, slot, color_grad, arrived)
    returned = exchange(returning)
    gh, gb, go, gob = region_backward(received, returned, wo_t, coef, encoded, layer)
    return (colour, gh[None], gb, go[None], gob)


def solution(mesh):
    spread = P(BOTH)
    in_specs = (
        P(None, BOTH),
        P(None, BOTH),
        spread,
        spread,
        P(None, BOTH),
        P(None, BOTH),
        spread,
        spread,
        spread,
        spread,
        spread,
    )
    out_specs = (P(None, BOTH), spread, spread, spread, spread)
    return jax.shard_map(
        shards, mesh=mesh, in_specs=in_specs, out_specs=out_specs, check_vma=False
    )
```
